128 devices in a mesh: seq: 8 (over z, core), exp: 16 (over y, x).
Axes of the slice: x: 4, y: 4, z: 4, core: 2. Of those that a mesh axis runs over, the one named last changes fastest.
Arguments:
- tokens: bfloat16 [16384, 2048], P(('seq', 'exp')), may hold values from -6 to 6
- norm_in: float32 [2048], replicated, may hold values from 0.1 to 1.9
- w_query: bfloat16 [2048, 2048], P(None, 'exp'), may hold values from -0.125 to 0.125
- w_key: bfloat16 [2048, 2048], P(None, 'exp'), may hold values from -0.125 to 0.125
- w_value: bfloat16 [2048, 4096], P(None, 'exp'), may hold values from -0.125 to 0.125
- w_outgate: bfloat16 [2048, 4096], P(None, 'exp'), may hold values from -0.125 to 0.125
- log_decay: float32 [32, 16384], P('exp', 'seq'), may hold values from -1 to 0, as said below
- write_rate: float32 [32, 16384], P('exp', 'seq'), may hold values from 0.005 to 0.95
- head_gain: float32 [128], replicated, may hold values from 0.1 to 1.9
- w_output: bfloat16 [4096, 2048], P('exp'), may hold values from -0.09375 to 0.09375
- norm_post: float32 [2048], replicated, may hold values from 0.1 to 1.9
- route_ids: int32 [16384, 10], P('seq'), may hold values from 0 to 31, all different within a row; in each aligned block of 128 rows (0 to 127, 128 to 255, ...) at most 80 rows name the same one
- route_weights: float32 [16384, 10], P('seq'), may hold values from 0.1 to 0.5
- w_gate: bfloat16 [32, 2048, 512], P('exp'), may hold values from -0.125 to 0.125
- w_up: bfloat16 [32, 2048, 512], P('exp'), may hold values from -0.125 to 0.125
- w_down: bfloat16 [32, 512, 2048], P('exp'), may hold values from -0.25 to 0.25
- w_shared_gate: bfloat16 [2048, 512], replicated, may hold values from -0.125 to 0.125
- w_shared_up: bfloat16 [2048, 512], replicated, may hold values from -0.125 to 0.125
- w_shared_down: bfloat16 [512, 2048], replicated, may hold values from -0.25 to 0.25
- w_shared_switch: bfloat16 [2048], replicated, may hold values from -0.125 to 0.125
Outputs:
- layer_out: bfloat16 [16384, 2048], P(('seq', 'exp'))
The draws below stay inside these ranges and needn't reach their ends.
Inputs may be any that keep to these rules, and one draw needn't show every extreme that they name: `route_ids`: each row names 10 different experts. In each aligned block of 128 rows (the tokens of one device) no expert is named by more than 80 rows. `log_decay`: never positive.
All inputs are finite; a program needn't handle non-finite values.
Results may differ from the reference program's by a relative error of at most 0.023.
Values may be sent and summed in bfloat16 or wider, within the bound.
No kernel may reach another device: no remote copies, remote signals or barrier semaphores. Data moves between devices by JAX's collectives and lax.ppermute only.
A program may use at most 192 MiB of HBM per device.

```python
import math
import jax
import jax.numpy as jnp
import numpy as np
from jax import lax

D = 2048
KHEADS = 16
VALUE_HEAD_COUNT = 32
DK = 128
DV = 128
MOE_FF = 512
SHARED_FF = 512
TOPK = 10
TOK_DEV = 128
TOK_SEQ = 2048
TOKEN_TOTAL = 16384
EXPERTS = 32
CAP = 80
N_EXP = 16


def head_kinds(key, share):
    return jax.random.bernoulli(key, share, (VALUE_HEAD_COUNT, 1))


def draw_log_decay(key, part):
    fast_share = 0.5
    fast_heads = head_kinds(key, fast_share)
    key = jax.random.fold_in(key, 7)
    random_subkeys = jax.random.split(key, 7)
    slow_rate = jnp.exp(jax.random.uniform(random_subkeys[1], (VALUE_HEAD_COUNT, 1), minval=jnp.log(0.1), maxval=jnp.log(0.6))) / TOKEN_TOTAL
    fast_rate = jnp.exp(-jax.random.uniform(random_subkeys[2], (VALUE_HEAD_COUNT, 1), minval=jnp.log(30.0), maxval=jnp.log(50.0)))
    decay_rates = jnp.where(fast_heads, fast_rate, slow_rate)
    partition_scale = jnp.exp(jax.random.uniform(random_subkeys[3], (VALUE_HEAD_COUNT, TOKEN_TOTAL // TOK_SEQ), minval=-0.7, maxval=0.7))
    partition_scale = jnp.repeat(partition_scale, TOK_SEQ, axis=1)
    jitter_amount = jax.random.uniform(random_subkeys[4], (VALUE_HEAD_COUNT, TOKEN_TOTAL), minval=0.5, maxval=1.5)
    spike_position = jax.random.randint(random_subkeys[5], (VALUE_HEAD_COUNT, 2, 1), 0, TOKEN_TOTAL)
    spike_events = jnp.any(spike_position == jnp.arange(TOKEN_TOTAL, dtype=jnp.int32)[None, None, :], axis=1)
    spike_log_value = jnp.log(jax.random.uniform(random_subkeys[6], (VALUE_HEAD_COUNT, TOKEN_TOTAL), minval=0.5, maxval=0.8))
    return (-decay_rates * partition_scale * jitter_amount + jnp.where(spike_events, spike_log_value, 0.0)).astype(jnp.float32)


def draw_write_rate(key, part):
    fast_share = 0.5
    slow_top = 0.08
    fast_heads = head_kinds(key, fast_share)
    key = jax.random.fold_in(key, 13)
    random_subkeys = jax.random.split(key, 2)
    fast_rate = jax.random.uniform(random_subkeys[0], (VALUE_HEAD_COUNT, TOKEN_TOTAL), minval=0.05, maxval=0.95)
    slow_rate = jnp.exp(jax.random.uniform(random_subkeys[1], (VALUE_HEAD_COUNT, TOKEN_TOTAL), minval=jnp.log(0.005), maxval=jnp.log(slow_top)))
    return jnp.where(fast_heads, fast_rate, slow_rate).astype(jnp.float32)


def block_levels(stream_key, dims, cuts, least, largest):
    loudness, own = 1.0, jax.random.fold_in(stream_key, 6)
    for dim, blocks in cuts:
        steps = jnp.exp(jax.random.uniform(jax.random.fold_in(own, dim), (blocks,), jnp.float32, least / len(cuts), largest / len(cuts)))
        loudness = loudness * jnp.repeat(steps, dims[dim] // blocks).reshape([-1 if axis == dim else 1 for axis in range(len(dims))])
    return loudness


def shared_out(stream_key, own, number, rows, number_of, top, bound, skew):
    sequence = jax.random.permutation(stream_key, number_of)
    packed, common = portions_of(number_of, rows * top, bound, skew, True), portions_of(number_of, rows * top, bound, skew, False)
    places = jnp.arange(number_of)

    def named(tallies, offset_by):
        used = int((tallies > 0).sum())
        fixed = max(1, used // 4)
        moved = fixed + (places - fixed + offset_by * (used - fixed)) % max(1, number_of - fixed)
        return jnp.zeros((number_of,), jnp.int32).at[sequence[jnp.where(places < fixed, places, moved)]].set(jnp.asarray(tallies, jnp.int32))

    tallies = jnp.where(number % 4 == 0, named(packed, number // 4), named(common, number - number // 4 - 1))
    mixed = jax.random.permutation(jax.random.fold_in(own, 3), number_of)
    source_of, taker = mixed[0:number_of // 2 * 2:2], mixed[1:number_of // 2 * 2:2]
    room = jnp.minimum(tallies[source_of] - 1, bound - tallies[taker]) // 2
    room = jnp.where((source_of == sequence[0]) | (taker == sequence[0]) | (tallies[taker] == 0), 0, jnp.maximum(room, 0))
    moved = jax.random.randint(jax.random.fold_in(own, 4), (number_of // 2,), 0, 1 << 20) % (room + 1)
    tallies = tallies.at[source_of].add(-moved).at[taker].add(moved)
    items = jnp.searchsorted(jnp.cumsum(tallies), jnp.arange(rows * top), side="right").astype(jnp.int32)
    table = items.reshape(top, rows).T
    table = table[jax.random.permutation(jax.random.fold_in(own, 1), rows)]
    offset_by = jax.random.randint(jax.random.fold_in(own, 2), (rows, 1), 0, top)
    return jnp.take_along_axis(table, (jnp.arange(top)[None, :] + offset_by) % top, axis=1)


def portions_of(count, total, limit, lean, full):
    loads = [(1 << 20) // math.isqrt(rank ** lean) + 1 for rank in range(1, count + 1)]
    largest = limit if full else min(limit, max(-(-total // count), total * loads[0] // sum(loads)))
    least = 1 if total - largest >= count - 1 else 0
    given, spare = [largest] + [least] * (count - 1), total - largest - least * (count - 1)
    while spare > 0:
        candidates = [i for i in range(1, count) if given[i] < largest] or [i for i in range(1, count) if given[i] < limit]
        mass, left = sum([loads[i] for i in candidates]), spare
        for i in candidates:
            more = min(limit - given[i], max(1, left * loads[i] // mass), spare)
            given[i] = given[i] + more
            spare = spare - more
    return np.array(given)


def scatter_about(key, dims, width, most, cuts=(), held_as=jnp.bfloat16):
    drawn = width * jax.random.normal(key, dims, jnp.float32)
    if cuts:
        drawn = drawn * block_levels(key, dims, cuts, -0.22, 0.18)
    return jnp.clip(drawn, -most, most).astype(held_as)


def setup_inputs(seed: int = 0) -> dict:
    key_list = jax.random.split(jax.random.key(seed), 21)
    tokens = scatter_about(key_list[0], (TOKEN_TOTAL, D), 1.0, 6.0, ((0, 128),))
    norm_in = jnp.clip(1.0 + 0.18 * jax.random.normal(key_list[1], (D,), jnp.float32), 0.1, 1.9)
    w_query = scatter_about(key_list[2], (D, KHEADS * DK), D ** -0.5, 0.125, ((1, 16),))
    w_key = scatter_about(key_list[3], (D, KHEADS * DK), D ** -0.5, 0.125, ((1, 16),))
    w_value = scatter_about(key_list[4], (D, VALUE_HEAD_COUNT * DV), D ** -0.5, 0.125, ((1, 16),))
    w_outgate = scatter_about(key_list[5], (D, VALUE_HEAD_COUNT * DV), D ** -0.5, 0.125, ((1, 16),))
    log_decay = draw_log_decay(jax.random.fold_in(key_list[20], 71), 0)
    write_rate = draw_write_rate(jax.random.fold_in(key_list[20], 71), 0)
    head_gain = jnp.clip(1.0 + 0.18 * jax.random.normal(key_list[8], (DV,), jnp.float32), 0.1, 1.9)
    w_output = scatter_about(key_list[9], (VALUE_HEAD_COUNT * DV, D), (VALUE_HEAD_COUNT * DV) ** -0.5, 0.09375, ((0, 16),))
    norm_post = jnp.clip(1.0 + 0.18 * jax.random.normal(key_list[10], (D,), jnp.float32), 0.1, 1.9)
    route_ids_keys = jax.random.split(jax.random.fold_in(key_list[11], 1), TOKEN_TOTAL // TOK_DEV)
    route_ids_turns = jax.random.permutation(jax.random.fold_in(key_list[11], 3), TOKEN_TOTAL // TOK_DEV)
    route_ids = jax.vmap(lambda own, number: shared_out(jax.random.fold_in(key_list[11], 2), own, number, TOK_DEV, EXPERTS, TOPK, CAP, 2))(route_ids_keys, route_ids_turns).reshape((TOKEN_TOTAL, TOPK))
    route_weights = jnp.clip(0.1 + 0.4 * jax.random.uniform(key_list[12], (TOKEN_TOTAL, TOPK), jnp.float32) ** block_levels(key_list[12], (TOKEN_TOTAL, TOPK), ((0, 8),), -0.2, 0.2), 0.1, 0.5)
    w_gate = scatter_about(key_list[13], (EXPERTS, D, MOE_FF), D ** -0.5, 0.125, ((0, 16),))
    w_up = scatter_about(key_list[14], (EXPERTS, D, MOE_FF), D ** -0.5, 0.125, ((0, 16),))
    w_down = scatter_about(key_list[15], (EXPERTS, MOE_FF, D), MOE_FF ** -0.5, 0.25, ((0, 16),))
    w_shared_gate = scatter_about(key_list[16], (D, SHARED_FF), D ** -0.5, 0.125)
    w_shared_up = scatter_about(key_list[17], (D, SHARED_FF), D ** -0.5, 0.125)
    w_shared_down = scatter_about(key_list[18], (SHARED_FF, D), SHARED_FF ** -0.5, 0.25)
    w_shared_switch = scatter_about(key_list[19], (D,), D ** -0.5, 0.125)
    return {"tokens": tokens, "norm_in": norm_in, "w_query": w_query, "w_key": w_key, "w_value": w_value, "w_outgate": w_outgate, "log_decay": log_decay, "write_rate": write_rate, "head_gain": head_gain, "w_output": w_output, "norm_post": norm_post, "route_ids": route_ids, "route_weights": route_weights, "w_gate": w_gate, "w_up": w_up, "w_down": w_down, "w_shared_gate": w_shared_gate, "w_shared_up": w_shared_up, "w_shared_down": w_shared_down, "w_shared_switch": w_shared_switch}


largest_value = lax.Precision.HIGHEST

def row_norm(values, gain_vec, epsilon):
    return values * lax.rsqrt(lax.optimization_barrier(jnp.mean(values * values, axis=-1, keepdims=True)) + epsilon) * gain_vec

def unit_rows(values):
    return values * lax.rsqrt(lax.optimization_barrier(jnp.sum(values * values, axis=-1, keepdims=True)) + 1e-06)

def block_terms(queries, key_rows, values, log_rates, strengths):
    length = queries.shape[-2]
    positions = jnp.arange(length, dtype=jnp.int32)
    causal = positions[:, None] >= positions[None, :]
    strict = positions[:, None] > positions[None, :]
    cumulative = jnp.cumsum(log_rates, axis=-1)
    spread_log = cumulative[..., :, None] - cumulative[..., None, :]
    ratios = jnp.where(causal, jnp.exp(jnp.where(causal, spread_log, 0.0)), 0.0)
    key_key = jnp.einsum('...td,...sd->...ts', key_rows, key_rows, precision=largest_value)
    query_key = jnp.einsum('...td,...sd->...ts', queries, key_rows, precision=largest_value)
    lower_part = jnp.where(strict, ratios * key_key * strengths[..., None, :], 0.0)
    identity = jnp.eye(length, dtype=jnp.float32)
    decays = jnp.exp(cumulative)
    stacked = jnp.concatenate([values, decays[..., None] * key_rows], axis=-1)
    solved = jax.scipy.linalg.solve_triangular(identity + lower_part, stacked, lower=True, unit_diagonal=True)
    value_width = values.shape[-1]
    updates = solved[..., :value_width]
    weights = solved[..., value_width:]
    mixing = ratios * query_key * strengths[..., None, :]
    local_out = jnp.einsum('...ts,...sv->...tv', mixing, updates, precision=largest_value)
    query_eff = decays[..., None] * queries - jnp.einsum('...ts,...sk->...tk', mixing, weights, precision=largest_value)
    to_end = jnp.exp(cumulative[..., -1:] - cumulative) * strengths
    key_tail = key_rows * to_end[..., None]
    key_width = key_rows.shape[-1]
    transit = decays[..., -1, None, None] * jnp.eye(key_width, dtype=jnp.float32) - jnp.einsum('...tk,...tl->...kl', key_tail, weights, precision=largest_value)
    inject = jnp.einsum('...tk,...tv->...kv', key_tail, updates, precision=largest_value)
    return (local_out, query_eff, transit, inject)

def run_blocks(current_state, local_out, query_eff, transit, inject):

    def advance(running_total, per_block):
        output_part, effective_part, transfer_part, addition_part = per_block
        final_result = output_part + jnp.einsum('rjw,rwe->rje', effective_part, running_total, precision=largest_value)
        running_total = jnp.einsum('eca,eaj->ecj', transfer_part, running_total, precision=largest_value) + addition_part
        return (running_total, final_result)
    per_block = (jnp.moveaxis(local_out, 1, 0), jnp.moveaxis(query_eff, 1, 0), jnp.moveaxis(transit, 1, 0), jnp.moveaxis(inject, 1, 0))
    final_state, outputs = lax.scan(advance, current_state, per_block)
    return jnp.moveaxis(outputs, 0, 1)

def slot_table(flat_rows, experts, capacity):
    flat_ids = flat_rows.reshape(-1)
    onehot = (flat_ids[:, None] == jnp.arange(experts, dtype=jnp.int32)[None, :]).astype(jnp.int32)
    slot_rank = lax.optimization_barrier(jnp.sum((jnp.cumsum(onehot, axis=0, dtype=jnp.int32) - onehot) * onehot, axis=1, dtype=jnp.int32))
    targets = flat_ids * capacity + slot_rank
    entries = jnp.arange(flat_ids.shape[0], dtype=jnp.int32)
    inverse = jnp.full((experts * capacity,), -1, jnp.int32).at[targets].set(entries)
    return (inverse, targets)

def expert_rows(inputs, gate_w, up_w, down_w):
    gate_part = jnp.dot(inputs.astype(jnp.float32), gate_w.astype(jnp.float32), preferred_element_type=jnp.float32)
    up_part = jnp.dot(inputs.astype(jnp.float32), up_w.astype(jnp.float32), preferred_element_type=jnp.float32)
    hidden = (jax.nn.silu(gate_part) * up_part).astype(jnp.bfloat16)
    return jnp.dot(hidden.astype(jnp.float32), down_w.astype(jnp.float32), preferred_element_type=jnp.float32).astype(jnp.bfloat16)

def reference(tokens, norm_in, w_query, w_key, w_value, w_outgate, log_decay, write_rate, head_gain, w_output, norm_post, route_ids, route_weights, w_gate, w_up, w_down, w_shared_gate, w_shared_up, w_shared_down, w_shared_switch):
    residual_in = tokens.astype(jnp.float32)
    normed = row_norm(residual_in, norm_in, 1e-06).astype(jnp.bfloat16)
    group_size = VALUE_HEAD_COUNT // KHEADS
    query_raw = jnp.dot(normed.astype(jnp.float32), w_query.astype(jnp.float32), preferred_element_type=jnp.float32).reshape(TOKEN_TOTAL, KHEADS, DK)
    key_raw = jnp.dot(normed.astype(jnp.float32), w_key.astype(jnp.float32), preferred_element_type=jnp.float32).reshape(TOKEN_TOTAL, KHEADS, DK)
    queries = jnp.transpose(jnp.repeat(query_raw, group_size, axis=1), (1, 0, 2))
    key_rows = jnp.transpose(jnp.repeat(unit_rows(key_raw), group_size, axis=1), (1, 0, 2))
    values = jnp.transpose(jnp.dot(normed.astype(jnp.float32), w_value.astype(jnp.float32), preferred_element_type=jnp.float32).reshape(TOKEN_TOTAL, VALUE_HEAD_COUNT, DV), (1, 0, 2))
    gate_proj = jnp.dot(normed.astype(jnp.float32), w_outgate.astype(jnp.float32), preferred_element_type=jnp.float32).reshape(TOKEN_TOTAL, VALUE_HEAD_COUNT, DV)
    length = min(128, TOK_SEQ)
    blocks = TOKEN_TOTAL // length

    def one_head(per_head):
        head_q, head_k, head_v, head_rates, head_strength = per_head
        block_parts = block_terms(head_q.reshape(1, blocks, length, DK), head_k.reshape(1, blocks, length, DK), head_v.reshape(1, blocks, length, DV), head_rates.reshape(1, blocks, length), head_strength.reshape(1, blocks, length))
        current_state = jnp.zeros((1, DK, DV), jnp.float32)
        return run_blocks(current_state, *block_parts).reshape(TOKEN_TOTAL, DV)
    attended = lax.map(one_head, (queries, key_rows, values, log_decay, write_rate))
    attended = jnp.transpose(attended, (1, 0, 2))
    gated = (row_norm(attended, head_gain, 1e-06) * jax.nn.silu(gate_proj)).astype(jnp.bfloat16)
    span_cols = VALUE_HEAD_COUNT * DV // N_EXP
    grouped = jnp.transpose(gated.reshape(TOKEN_TOTAL, N_EXP, span_cols), (1, 0, 2))
    out_groups = w_output.reshape(N_EXP, span_cols, D)

    def add_group(running_sum, per_group):
        group_in, group_w = per_group
        term_now = jnp.dot(group_in.astype(jnp.float32), group_w.astype(jnp.float32), preferred_element_type=jnp.float32).astype(jnp.bfloat16)
        term_now = lax.optimization_barrier(term_now)
        return (running_sum + term_now.astype(jnp.float32), None)
    mixed_out, _ = lax.scan(add_group, jnp.zeros((TOKEN_TOTAL, D), jnp.float32), (grouped, out_groups))
    residual = residual_in + mixed_out
    post_norm = row_norm(residual, norm_post, 1e-06).astype(jnp.bfloat16)
    switch = jax.nn.sigmoid(jnp.dot(post_norm.astype(jnp.float32), w_shared_switch.astype(jnp.float32), preferred_element_type=jnp.float32))
    inner_act = (jax.nn.silu(jnp.dot(post_norm.astype(jnp.float32), w_shared_gate.astype(jnp.float32), preferred_element_type=jnp.float32)) * jnp.dot(post_norm.astype(jnp.float32), w_shared_up.astype(jnp.float32), preferred_element_type=jnp.float32)).astype(jnp.bfloat16)
    shared = jnp.dot(inner_act.astype(jnp.float32), w_shared_down.astype(jnp.float32), preferred_element_type=jnp.float32) * switch[:, None]
    block_count = TOKEN_TOTAL // TOK_DEV

    def table_of(block_ids):
        return slot_table(block_ids, EXPERTS, CAP)
    inverse_all, _ = jax.vmap(table_of)(route_ids.reshape(block_count, TOK_DEV, TOPK))
    flat_weights = route_weights.reshape(block_count, TOK_DEV * TOPK)
    block_base = (jnp.arange(block_count, dtype=jnp.int32) * TOK_DEV)[:, None]

    def add_expert(running_sum, expert):
        row_ids = lax.dynamic_slice_in_dim(inverse_all, expert * CAP, CAP, 1)
        present = row_ids >= 0
        clipped = jnp.maximum(row_ids, 0)
        token_at = (block_base + clipped // TOPK).reshape(-1)
        scaling = jnp.where(present, jnp.take_along_axis(flat_weights, clipped, axis=1), 0.0).reshape(-1, 1)
        produced = expert_rows(post_norm[token_at], w_gate[expert], w_up[expert], w_down[expert])
        return (running_sum.at[token_at].add(scaling * produced.astype(jnp.float32)), None)
    routed, _ = lax.scan(add_expert, jnp.zeros((TOKEN_TOTAL, D), jnp.float32), jnp.arange(EXPERTS, dtype=jnp.int32))
    return (residual + shared + routed).astype(jnp.bfloat16)
```

```python
import jax
import jax.numpy as jnp
from jax import lax
from jax.experimental import pallas as pl
from jax.experimental.pallas import tpu as pltpu
from jax.sharding import PartitionSpec as P

DK = 128
DV = 128
BLOCK = 128
F32 = jnp.float32
BF16 = jnp.bfloat16
NN = (((1,), (0,)), ((), ()))
NT = (((1,), (1,)), ((), ()))
TN = (((0,), (0,)), ((), ()))


def row_norm(values, gain_vec, epsilon):
    return (
        values * lax.rsqrt(jnp.mean(values * values, axis=-1, keepdims=True) + epsilon) * gain_vec
    )


def split(x):
    hi = x.astype(BF16)
    return hi, (x - hi.astype(F32)).astype(BF16)


def mm(a, b, dims=NN):
    return lax.dot_general(a, b, dims, preferred_element_type=F32)


def dot3_narrow(a, b):
    ah, al = split(a)
    bh, bl = split(b)
    left = jnp.concatenate([ah, al], axis=1)
    right = jnp.concatenate(
        [jnp.concatenate([bh, bl], axis=1), jnp.concatenate([bh, jnp.zeros_like(bl)], axis=1)],
        axis=0,
    )
    both = mm(left, right)
    return both[:, :128] + both[:, 128:]


def dot3_wide(a, b):
    ah, al = split(a)
    bh, bl = split(b)
    return mm(jnp.concatenate([ah, al], axis=1), jnp.concatenate([bh, bh], axis=0)) + mm(ah, bl)


def delta_kernel(blocks, proj_ref, cum_ref, rate_ref, base_ref, reach_ref, total_ref, state):
    step = pl.program_id(0)
    rows = lax.broadcasted_iota(jnp.int32, (BLOCK, BLOCK), 0)
    cols = lax.broadcasted_iota(jnp.int32, (BLOCK, BLOCK), 1)
    causal = rows >= cols
    strict = rows > cols
    apart = rows ^ cols
    eye = jnp.where(rows == cols, 1.0, 0.0).astype(F32)
    heads = 2

    @pl.when(step == 0)
    def _():
        for h in range(heads):
            state[h] = jnp.concatenate([eye, jnp.zeros((DK, DV), F32)], axis=1)

    problems = []
    for b in range(blocks):
        span = slice(b * BLOCK, (b + 1) * BLOCK)
        query = proj_ref[span, 0:DK]
        key = proj_ref[span, DK : 2 * DK]
        key = key * lax.rsqrt(jnp.sum(key * key, axis=-1, keepdims=True) + 1e-06)
        qh, ql = split(query)
        kh, kl = split(key)
        stacked_h = jnp.concatenate([kh, qh], axis=0)
        stacked_l = jnp.concatenate([kl, ql], axis=0)
        products = mm(stacked_h, kh, NT) + (mm(stacked_h, kl, NT) + mm(stacked_l, kh, NT))
        key_key, query_key = products[:BLOCK], products[BLOCK:]
        for h in range(heads):
            cum_row = jnp.broadcast_to(cum_ref[h, b : b + 1, :], (BLOCK, BLOCK))
            rate_row = jnp.broadcast_to(rate_ref[h, b : b + 1, :], (BLOCK, BLOCK))
            cum_col = cum_row.T
            rate_col = rate_row.T
            ratios = jnp.where(causal, jnp.exp(jnp.where(causal, cum_col - cum_row, 0.0)), 0.0)
            weighted = ratios * rate_row
            lower = jnp.where(strict, weighted * key_key, 0.0)
            mixing = weighted * query_key
            decays = jnp.exp(cum_col)
            last = cum_col[BLOCK - 1 : BLOCK, :]
            key_tail = key * (jnp.exp(last - cum_col) * rate_col)
            value = proj_ref[span, 2 * DK + h * DV : 2 * DK + (h + 1) * DV]
            problems.append(
                dict(
                    b=b,
                    h=h,
                    lower=lower,
                    mixing=mixing,
                    right=jnp.concatenate([value, decays * key], axis=1),
                    query=decays * query,
                    key_tail=key_tail,
                    fade=jnp.exp(last) * eye,
                    inverse=eye - jnp.where(apart == 1, lower, 0.0),
                )
            )
    size = 2
    while size < BLOCK:
        for p in problems:
            part = jnp.where((apart >= size) & (apart < 2 * size), p["lower"], 0.0)
            p["inner"] = dot3_narrow(part, p["inverse"])
        for p in problems:
            p["inverse"] = p["inverse"] - dot3_narrow(p["inverse"], p["inner"])
        size *= 2
    for p in problems:
        p["solved"] = dot3_wide(p["inverse"], p["right"])
    for p in problems:
        p["mixed"] = dot3_wide(p["mixing"], p["solved"])
        p["tail"] = dot3_wide(p["key_tail"].T, p["solved"])
    for p in problems:
        h = p["h"]
        span = slice(p["b"] * BLOCK, (p["b"] + 1) * BLOCK)
        cols_h = slice(h * DV, (h + 1) * DV)
        before = state[h]
        effective = p["query"] - p["mixed"][:, DV:]
        seen = dot3_wide(effective, before)
        reach_ref[span, cols_h] = seen[:, :DK]
        base_ref[span, cols_h] = p["mixed"][:, :DV] + seen[:, DK:]
        moved = dot3_wide(p["fade"] - p["tail"][:, DV:], before)
        state[h] = jnp.concatenate([moved[:, :DK], moved[:, DK:] + p["tail"][:, :DV]], axis=1)

    @pl.when(step == pl.num_programs(0) - 1)
    def _():
        total_ref[...] = state[...].astype(total_ref.dtype)


def delta_local(proj, cumulative, rates):
    tokens = proj.shape[0]
    blocks = 8
    steps = tokens // (blocks * BLOCK)
    return pl.pallas_call(
        lambda *refs: delta_kernel(blocks, *refs),
        grid=(steps,),
        in_specs=[
            pl.BlockSpec((blocks * BLOCK, 2 * DK + 2 * DV), lambda i: (i, 0)),
            pl.BlockSpec((2, blocks, BLOCK), lambda i: (0, i, 0)),
            pl.BlockSpec((2, blocks, BLOCK), lambda i: (0, i, 0)),
        ],
        out_specs=[
            pl.BlockSpec((blocks * BLOCK, 2 * DV), lambda i: (i, 0)),
            pl.BlockSpec((blocks * BLOCK, 2 * DV), lambda i: (i, 0)),
            pl.BlockSpec((2, DK, DK + DV), lambda i: (0, 0, 0)),
        ],
        out_shape=[
            jax.ShapeDtypeStruct((tokens, 2 * DV), F32),
            jax.ShapeDtypeStruct((tokens, 2 * DV), F32),
            jax.ShapeDtypeStruct((2, DK, DK + DV), BF16),
        ],
        scratch_shapes=[pltpu.VMEM((2, DK, DK + DV), F32)],
        compiler_params=pltpu.CompilerParams(vmem_limit_bytes=40 * 2**20),
        name="delta_local",
    )(proj, cumulative, rates)


def gate_kernel(stretches, place_ref, totals_ref, base_ref, reach_ref, gate_ref, gain_ref, out_ref, entering):
    @pl.when(pl.program_id(0) == 0)
    def _():
        for h in range(2):
            entering[h] = jnp.zeros((DK, DV), F32)
        for j in range(stretches - 1):
            before = j < place_ref[0]
            for h in range(2):
                pair = totals_ref[j, h]
                high, low = split(entering[h])
                moved = mm(pair[:, :DK], jnp.concatenate([high, low], axis=1))
                moved = moved[:, :DV] + moved[:, DV:] + pair[:, DK:].astype(F32)
                entering[h] = jnp.where(before, moved, entering[h])

    for h in range(2):
        span = slice(h * DV, (h + 1) * DV)
        attended = base_ref[:, span] + dot3_narrow(reach_ref[:, span], entering[h])
        scaled = row_norm(attended, gain_ref[...], 1e-06)
        u = gate_ref[:, span]
        out_ref[:, span] = (scaled * (u / (1.0 + jnp.exp(-u)))).astype(out_ref.dtype)


def delta_gate(place, totals, base, reach, proj, gain):
    tokens = base.shape[0]
    rows = 512
    stretches = totals.shape[0]
    return pl.pallas_call(
        lambda *refs: gate_kernel(stretches, *refs),
        grid_spec=pltpu.PrefetchScalarGridSpec(
            num_scalar_prefetch=1,
            grid=(tokens // rows,),
            in_specs=[
                pl.BlockSpec((stretches, 2, DK, DK + DV), lambda i, s: (0, 0, 0, 0)),
                pl.BlockSpec((rows, 2 * DV), lambda i, s: (i, 0)),
                pl.BlockSpec((rows, 2 * DV), lambda i, s: (i, 0)),
                pl.BlockSpec((rows, 2 * DV), lambda i, s: (i, 2)),
                pl.BlockSpec((1, DV), lambda i, s: (0, 0)),
            ],
            out_specs=pl.BlockSpec((rows, 2 * DV), lambda i, s: (i, 0)),
            scratch_shapes=[pltpu.VMEM((2, DK, DV), F32)],
        ),
        out_shape=jax.ShapeDtypeStruct((tokens, 2 * DV), BF16),
        compiler_params=pltpu.CompilerParams(vmem_limit_bytes=40 * 2**20),
        name="delta_gate",
    )(place, totals, base, reach, proj, gain)


def expert_kernel(x_ref, share_ref, gate_ref, up_ref, down_ref, out_ref):
    x = x_ref[...]
    total = None
    for j in range(gate_ref.shape[0]):
        gated = mm(x, gate_ref[j])
        raised = mm(x, up_ref[j])
        hidden = gated / (1.0 + jnp.exp(-gated)) * raised * share_ref[:, j : j + 1]
        made = mm(hidden.astype(BF16), down_ref[j])
        total = made if total is None else total + made
    out_ref[...] = total.astype(out_ref.dtype)


def expert_mix(x, shares, w_gate, w_up, w_down):
    tokens, width = x.shape
    count, _, inner = w_gate.shape
    rows = 256
    whole = lambda i: (0, 0, 0)
    return pl.pallas_call(
        expert_kernel,
        grid=(tokens // rows,),
        in_specs=[
            pl.BlockSpec((rows, width), lambda i: (i, 0)),
            pl.BlockSpec((rows, count), lambda i: (i, 0)),
            pl.BlockSpec((count, width, inner), whole, pipeline_mode=pl.Buffered(1)),
            pl.BlockSpec((count, width, inner), whole, pipeline_mode=pl.Buffered(1)),
            pl.BlockSpec((count, inner, width), whole, pipeline_mode=pl.Buffered(1)),
        ],
        out_specs=pl.BlockSpec((rows, width), lambda i: (i, 0)),
        out_shape=jax.ShapeDtypeStruct((tokens, width), BF16),
        compiler_params=pltpu.CompilerParams(vmem_limit_bytes=48 * 2**20),
        name="expert_mix",
    )(x, shares, w_gate, w_up, w_down)


def local(
    tokens,
    norm_in,
    w_query,
    w_key,
    w_value,
    w_outgate,
    log_decay,
    write_rate,
    head_gain,
    w_output,
    norm_post,
    route_ids,
    route_weights,
    w_gate,
    w_up,
    w_down,
    w_shared_gate,
    w_shared_up,
    w_shared_down,
    w_shared_switch,
):
    tok_dev = tokens.shape[0]
    owners = lax.axis_size("exp")
    tok_seq = tok_dev * owners
    position = lax.axis_index("exp")
    residual_in = tokens.astype(F32)
    normed = row_norm(residual_in, norm_in, 1e-06).astype(BF16)
    w_all = jnp.concatenate([w_query, w_key, w_value, w_outgate], axis=1)
    projected = jnp.dot(
        lax.all_gather(normed, "exp", axis=0, tiled=True), w_all, preferred_element_type=F32
    )
    blocks = tok_seq // BLOCK
    cumulative = jnp.cumsum(log_decay.reshape(2, blocks, BLOCK), axis=-1)
    base, reach, total = delta_local(projected, cumulative, write_rate.reshape(2, blocks, BLOCK))
    totals = lax.all_gather(total, "seq", axis=0)
    place = lax.axis_index("seq").astype(jnp.int32).reshape(1)
    gated = delta_gate(place, totals, base, reach, projected, head_gain.reshape(1, DV))
    mixed_out = lax.psum_scatter(
        jnp.dot(gated, w_output, preferred_element_type=F32).astype(BF16),
        "exp",
        scatter_dimension=0,
        tiled=True,
    ).astype(F32)
    residual = residual_in + mixed_out
    post_norm = row_norm(residual, norm_post, 1e-06).astype(BF16)
    everyone = lax.all_gather(post_norm, "exp", axis=0, tiled=True)
    switch = jax.nn.sigmoid(jnp.dot(post_norm, w_shared_switch, preferred_element_type=F32))
    inner_act = (
        jax.nn.silu(jnp.dot(post_norm, w_shared_gate, preferred_element_type=F32))
        * jnp.dot(post_norm, w_shared_up, preferred_element_type=F32)
    ).astype(BF16)
    shared = jnp.dot(inner_act, w_shared_down, preferred_element_type=F32) * switch[:, None]
    count = w_gate.shape[0]
    mine = position * count + jnp.arange(count, dtype=jnp.int32)
    shares = jnp.sum(
        jnp.where(route_ids[:, :, None] == mine, route_weights[:, :, None], 0.0), axis=1
    )
    made = expert_mix(everyone, shares, w_gate, w_up, w_down)
    routed = lax.psum_scatter(made, "exp", scatter_dimension=0, tiled=True).astype(F32)
    return (residual + shared + routed).astype(BF16)


def solution(mesh):
    in_specs = (
        P(("seq", "exp"), None),
        P(),
        P(None, "exp"),
        P(None, "exp"),
        P(None, "exp"),
        P(None, "exp"),
        P("exp", "seq"),
        P("exp", "seq"),
        P(),
        P("exp", None),
        P(),
        P("seq", None),
        P("seq", None),
        P("exp", None, None),
        P("exp", None, None),
        P("exp", None, None),
        P(),
        P(),
        P(),
        P(),
    )
    out_specs = P(("seq", "exp"), None)
    return jax.shard_map(local, mesh=mesh, in_specs=in_specs, out_specs=out_specs, check_vma=False)
```

```python
import jax
import jax.numpy as jnp
from jax import lax
from jax.experimental import pallas as pl
from jax.experimental.pallas import tpu as pltpu
from jax.sharding import PartitionSpec as P

DK = 128
DV = 128
BLOCK = 128
F32 = jnp.float32
BF16 = jnp.bfloat16
NN = (((1,), (0,)), ((), ()))
NT = (((1,), (1,)), ((), ()))
TN = (((0,), (0,)), ((), ()))


def row_norm(values, gain_vec, epsilon):
    return (
        values * lax.rsqrt(jnp.mean(values * values, axis=-1, keepdims=True) + epsilon) * gain_vec
    )


def split(x):
    hi = x.astype(BF16)
    return hi, (x - hi.astype(F32)).astype(BF16)


def mm(a, b, dims=NN):
    return lax.dot_general(a, b, dims, preferred_element_type=F32)


def dot3_narrow(a, b):
    ah, al = split(a)
    bh, bl = split(b)
    left = jnp.concatenate([ah, al], axis=1)
    right = jnp.concatenate(
        [jnp.concatenate([bh, bl], axis=1), jnp.concatenate([bh, jnp.zeros_like(bl)], axis=1)],
        axis=0,
    )
    both = mm(left, right)
    return both[:, :128] + both[:, 128:]


def dot3_wide(a, b):
    ah, al = split(a)
    bh, bl = split(b)
    return mm(jnp.concatenate([ah, al], axis=1), jnp.concatenate([bh, bh], axis=0)) + mm(ah, bl)


def delta_kernel(blocks, proj_ref, cum_ref, rate_ref, base_ref, reach_ref, total_ref, state):
    step = pl.program_id(0)
    rows = lax.broadcasted_iota(jnp.int32, (BLOCK, BLOCK), 0)
    cols = lax.broadcasted_iota(jnp.int32, (BLOCK, BLOCK), 1)
    causal = rows >= cols
    strict = rows > cols
    apart = rows ^ cols
    eye = jnp.where(rows == cols, 1.0, 0.0).astype(F32)
    heads = 2

    @pl.when(step == 0)
    def _():
        for h in range(heads):
            state[h] = jnp.concatenate([eye, jnp.zeros((DK, DV), F32)], axis=1)

    problems = []
    for b in range(blocks):
        span = slice(b * BLOCK, (b + 1) * BLOCK)
        query = proj_ref[span, 0:DK]
        key = proj_ref[span, DK : 2 * DK]
        key = key * lax.rsqrt(jnp.sum(key * key, axis=-1, keepdims=True) + 1e-06)
        qh, ql = split(query)
        kh, kl = split(key)
        stacked_h = jnp.concatenate([kh, qh], axis=0)
        stacked_l = jnp.concatenate([kl, ql], axis=0)
        products = mm(stacked_h, kh, NT) + (mm(stacked_h, kl, NT) + mm(stacked_l, kh, NT))
        key_key, query_key = products[:BLOCK], products[BLOCK:]
        for h in range(heads):
            cum_row = jnp.broadcast_to(cum_ref[h, b : b + 1, :], (BLOCK, BLOCK))
            rate_row = jnp.broadcast_to(rate_ref[h, b : b + 1, :], (BLOCK, BLOCK))
            cum_col = cum_row.T
            rate_col = rate_row.T
            ratios = jnp.where(causal, jnp.exp(jnp.where(causal, cum_col - cum_row, 0.0)), 0.0)
            weighted = ratios * rate_row
            lower = jnp.where(strict, weighted * key_key, 0.0)
            mixing = weighted * query_key
            decays = jnp.exp(cum_col)
            last = cum_col[BLOCK - 1 : BLOCK, :]
            key_tail = key * (jnp.exp(last - cum_col) * rate_col)
            value = proj_ref[span, 2 * DK + h * DV : 2 * DK + (h + 1) * DV]
            problems.append(
                dict(
                    b=b,
                    h=h,
                    lower=lower,
                    mixing=mixing,
                    right=jnp.concatenate([value, decays * key], axis=1),
                    query=decays * query,
                    key_tail=key_tail,
                    fade=jnp.exp(last) * eye,
                    inverse=eye - jnp.where(apart == 1, lower, 0.0),
                )
            )
    size = 2
    while size < BLOCK:
        for p in problems:
            part = jnp.where((apart >= size) & (apart < 2 * size), p["lower"], 0.0)
            p["inner"] = dot3_narrow(part, p["inverse"])
        for p in problems:
            p["inverse"] = p["inverse"] - dot3_narrow(p["inverse"], p["inner"])
        size *= 2
    for p in problems:
        p["solved"] = dot3_wide(p["inverse"], p["right"])
    for p in problems:
        p["mixed"] = dot3_wide(p["mixing"], p["solved"])
        p["tail"] = dot3_wide(p["key_tail"].T, p["solved"])
    for p in problems:
        h = p["h"]
        span = slice(p["b"] * BLOCK, (p["b"] + 1) * BLOCK)
        cols_h = slice(h * DV, (h + 1) * DV)
        before = state[h]
        effective = p["query"] - p["mixed"][:, DV:]
        seen = dot3_wide(effective, before)
        reach_ref[span, cols_h] = seen[:, :DK]
        base_ref[span, cols_h] = p["mixed"][:, :DV] + seen[:, DK:]
        moved = dot3_wide(p["fade"] - p["tail"][:, DV:], before)
        state[h] = jnp.concatenate([moved[:, :DK], moved[:, DK:] + p["tail"][:, :DV]], axis=1)

    @pl.when(step == pl.num_programs(0) - 1)
    def _():
        total_ref[...] = state[...].astype(total_ref.dtype)


def delta_local(proj, cumulative, rates):
    tokens = proj.shape[0]
    blocks = 8
    steps = tokens // (blocks * BLOCK)
    return pl.pallas_call(
        lambda *refs: delta_kernel(blocks, *refs),
        grid=(steps,),
        in_specs=[
            pl.BlockSpec((blocks * BLOCK, 2 * DK + 2 * DV), lambda i: (i, 0)),
            pl.BlockSpec((2, blocks, BLOCK), lambda i: (0, i, 0)),
            pl.BlockSpec((2, blocks, BLOCK), lambda i: (0, i, 0)),
        ],
        out_specs=[
            pl.BlockSpec((blocks * BLOCK, 2 * DV), lambda i: (i, 0)),
            pl.BlockSpec((blocks * BLOCK, 2 * DV), lambda i: (i, 0)),
            pl.BlockSpec((2, DK, DK + DV), lambda i: (0, 0, 0)),
        ],
        out_shape=[
            jax.ShapeDtypeStruct((tokens, 2 * DV), F32),
            jax.ShapeDtypeStruct((tokens, 2 * DV), F32),
            jax.ShapeDtypeStruct((2, DK, DK + DV), BF16),
        ],
        scratch_shapes=[pltpu.VMEM((2, DK, DK + DV), F32)],
        compiler_params=pltpu.CompilerParams(vmem_limit_bytes=60 * 2**20),
        name="delta_local",
    )(proj, cumulative, rates)


def gate_kernel(
    stretches, place_ref, totals_ref, base_ref, reach_ref, gate_ref, gain_ref, first_ref, second_ref, entering
):
    @pl.when(pl.program_id(0) == 0)
    def _():
        for h in range(2):
            entering[h] = jnp.zeros((DK, DV), F32)
        for j in range(stretches - 1):
            before = j < place_ref[0]
            for h in range(2):
                pair = totals_ref[j, h]
                high, low = split(entering[h])
                moved = mm(pair[:, :DK], jnp.concatenate([high, low], axis=1))
                moved = moved[:, :DV] + moved[:, DV:] + pair[:, DK:].astype(F32)
                entering[h] = jnp.where(before, moved, entering[h])

    rows = base_ref.shape[0] // SIDE
    for h in range(2):
        span = slice(h * DV, (h + 1) * DV)
        attended = base_ref[:, span] + dot3_narrow(reach_ref[:, span], entering[h])
        scaled = row_norm(attended, gain_ref[...], 1e-06)
        u = gate_ref[:, span]
        gated = (scaled * (u / (1.0 + jnp.exp(-u)))).astype(first_ref.dtype)
        for x in range(SIDE):
            away = lax.rem(x - place_ref[2] + SIDE, SIDE)
            start = x * rows
            first_ref[0, away, :, span] = gated[start : start + rows // 2]
            second_ref[away, 0, :, span] = gated[start + rows // 2 : start + rows]


def delta_gate(place, totals, base, reach, proj, gain):
    tokens = base.shape[0]
    rows = tokens // SIDE
    part = rows // SIDE // 2
    stretches = totals.shape[0]
    away = lambda i, p: lax.rem(i - p[1] + SIDE, SIDE)
    return pl.pallas_call(
        lambda *refs: gate_kernel(stretches, *refs),
        grid_spec=pltpu.PrefetchScalarGridSpec(
            num_scalar_prefetch=1,
            grid=(SIDE,),
            in_specs=[
                pl.BlockSpec((stretches, 2, DK, DK + DV), lambda i, p: (0, 0, 0, 0)),
                pl.BlockSpec((rows, 2 * DV), lambda i, p: (i, 0)),
                pl.BlockSpec((rows, 2 * DV), lambda i, p: (i, 0)),
                pl.BlockSpec((rows, 2 * DV), lambda i, p: (i, 2)),
                pl.BlockSpec((1, DV), lambda i, p: (0, 0)),
            ],
            out_specs=[
                pl.BlockSpec((1, SIDE, part, 2 * DV), lambda i, p: (away(i, p), 0, 0, 0)),
                pl.BlockSpec((SIDE, 1, part, 2 * DV), lambda i, p: (0, away(i, p), 0, 0)),
            ],
            scratch_shapes=[pltpu.VMEM((2, DK, DV), F32)],
        ),
        out_shape=[jax.ShapeDtypeStruct((SIDE, SIDE, part, 2 * DV), BF16)] * 2,
        compiler_params=pltpu.CompilerParams(vmem_limit_bytes=60 * 2**20),
        name="delta_gate",
    )(place, totals, base, reach, proj, gain)


def expert_kernel(xa_ref, xb_ref, sa_ref, sb_ref, gate_ref, up_ref, down_ref, oa_ref, ob_ref, x_ref, total):
    width = xa_ref.shape[-1]
    rows = xa_ref.size // width
    step = pl.program_id(0)
    expert = step // EXPERT_CUTS

    @pl.when(step == 0)
    def _():
        x_ref[:rows] = xa_ref[...].reshape(rows, width)
        x_ref[rows:] = xb_ref[...].reshape(rows, width)

    x = x_ref[...]
    shares = jnp.concatenate(
        [sa_ref[...].reshape(rows, -1), sb_ref[...].reshape(rows, -1)], axis=0
    )
    share = jnp.where(expert == 0, shares[:, 0:1], shares[:, 1:2])
    gated = mm(x, gate_ref[0])
    raised = mm(x, up_ref[0])
    hidden = gated / (1.0 + jnp.exp(-gated)) * raised * share
    made = mm(hidden.astype(BF16), down_ref[0])

    @pl.when(step == 0)
    def _():
        total[...] = made

    @pl.when((step > 0) & (step < pl.num_programs(0) - 1))
    def _():
        total[...] += made

    @pl.when(step == pl.num_programs(0) - 1)
    def _():
        done = (total[...] + made).astype(oa_ref.dtype)
        oa_ref[...] = done[:rows].reshape(oa_ref.shape)
        ob_ref[...] = done[rows:].reshape(ob_ref.shape)


EXPERT_CUTS = 2


def expert_mix(xa, xb, sa, sb, w_gate, w_up, w_down):
    side, part, width = xa.shape
    count, _, inner = w_gate.shape
    cut = inner // EXPERT_CUTS
    whole = lambda i: (0, 0, 0)
    rows_spec = pl.BlockSpec((side, part, width), whole, pipeline_mode=pl.Buffered(1))
    share_spec = pl.BlockSpec((side, part, count), whole, pipeline_mode=pl.Buffered(1))
    out_spec = pl.BlockSpec((side, part, width), whole)
    across = pl.BlockSpec((1, width, cut), lambda i: (i // EXPERT_CUTS, 0, i % EXPERT_CUTS))
    down = pl.BlockSpec((1, cut, width), lambda i: (i // EXPERT_CUTS, i % EXPERT_CUTS, 0))
    return pl.pallas_call(
        expert_kernel,
        grid=(count * EXPERT_CUTS,),
        in_specs=[rows_spec, rows_spec, share_spec, share_spec, across, across, down],
        out_specs=[out_spec, out_spec],
        out_shape=[jax.ShapeDtypeStruct((side, part, width), BF16)] * 2,
        scratch_shapes=[
            pltpu.VMEM((2 * side * part, width), BF16),
            pltpu.VMEM((2 * side * part, width), F32),
        ],
        compiler_params=pltpu.CompilerParams(vmem_limit_bytes=48 * 2**20),
        cost_estimate=pl.CostEstimate(
            flops=12 * side * part * count * width * inner,
            bytes_accessed=6 * count * width * inner + 8 * side * part * width,
            transcendentals=2 * side * part * count * inner,
        ),
        name="expert_mix",
    )(xa, xb, sa, sb, w_gate, w_up, w_down)


SIDE = 4


def neighbour(value, axis, by):
    pairs = []
    for y in range(SIDE):
        for x in range(SIDE):
            ny, nx = ((y + by) % SIDE, x) if axis == 0 else (y, (x + by) % SIDE)
            pairs.append((y * SIDE + x, ny * SIDE + nx))
    return lax.ppermute(value, "exp", pairs)


def plus(*terms):
    total = terms[0].astype(F32)
    for term in terms[1:]:
        total = total + term.astype(F32)
    return total


def reduce_ring(groups, axis, final):
    far = groups(2)
    half = far.shape[0] // 2
    up = neighbour(far[:half], axis, 1)
    down = neighbour(far[half:], axis, -1)
    ahead, behind = groups(1), groups(-1)
    ahead = jnp.concatenate([plus(ahead[:half], up).astype(BF16), ahead[half:]], axis=0)
    behind = jnp.concatenate([behind[:half], plus(behind[half:], down).astype(BF16)], axis=0)
    from_behind = neighbour(ahead, axis, 1)
    from_ahead = neighbour(behind, axis, -1)
    return plus(groups(0), from_behind, from_ahead).astype(final)


def scatter_sums(first, second):
    a = reduce_ring(first, 0, BF16)
    b = reduce_ring(second, 1, BF16)
    a = reduce_ring(lambda k: a[k % SIDE], 1, F32)
    b = reduce_ring(lambda k: b[k % SIDE], 0, F32)
    return jnp.concatenate([a, b], axis=0)


def gather_ring(block, axis):
    half = block.shape[0] // 2
    behind = neighbour(block, axis, 1)
    ahead = neighbour(block, axis, -1)
    far = jnp.concatenate(
        [neighbour(behind[:half], axis, 1), neighbour(ahead[half:], axis, -1)], axis=0
    )
    return [block, ahead, far, behind]


def gather_rows(rows):
    part = rows.shape[0] // 2
    first = gather_ring(jnp.stack(gather_ring(rows[:part], 1)), 0)
    second = gather_ring(jnp.stack(gather_ring(rows[part:], 0)), 1)
    return first, second


def local(
    tokens,
    norm_in,
    w_query,
    w_key,
    w_value,
    w_outgate,
    log_decay,
    write_rate,
    head_gain,
    w_output,
    norm_post,
    route_ids,
    route_weights,
    w_gate,
    w_up,
    w_down,
    w_shared_gate,
    w_shared_up,
    w_shared_down,
    w_shared_switch,
):
    tok_dev = tokens.shape[0]
    owners = lax.axis_size("exp")
    tok_seq = tok_dev * owners
    position = lax.axis_index("exp")
    residual_in = tokens.astype(F32)
    normed = row_norm(residual_in, norm_in, 1e-06).astype(BF16)
    w_all = jnp.concatenate([w_query, w_key, w_value, w_outgate], axis=1)
    projected = jnp.dot(
        lax.all_gather(normed, "exp", axis=0, tiled=True), w_all, preferred_element_type=F32
    )
    blocks = tok_seq // BLOCK
    cumulative = jnp.cumsum(log_decay.reshape(2, blocks, BLOCK), axis=-1)
    base, reach, total = delta_local(projected, cumulative, write_rate.reshape(2, blocks, BLOCK))
    totals = lax.all_gather(total, "seq", axis=0)
    y, x = position // SIDE, position % SIDE
    place = jnp.stack([lax.axis_index("seq"), y, x]).astype(jnp.int32)
    gated = delta_gate(place, totals, base, reach, projected, head_gain.reshape(1, DV))

    def out_terms(rows):
        made = jnp.dot(rows.reshape(-1, rows.shape[-1]), w_output, preferred_element_type=F32)
        return made.astype(BF16).reshape(rows.shape[0], rows.shape[1], -1)

    mixed_out = scatter_sums(
        lambda k: out_terms(gated[0][k % SIDE]), lambda k: out_terms(gated[1][k % SIDE])
    )
    residual = residual_in + mixed_out
    post_norm = row_norm(residual, norm_post, 1e-06).astype(BF16)
    firsts, seconds = gather_rows(post_norm)
    switch = jax.nn.sigmoid(jnp.dot(post_norm, w_shared_switch, preferred_element_type=F32))
    inner_act = (
        jax.nn.silu(jnp.dot(post_norm, w_shared_gate, preferred_element_type=F32))
        * jnp.dot(post_norm, w_shared_up, preferred_element_type=F32)
    ).astype(BF16)
    shared = jnp.dot(inner_act, w_shared_down, preferred_element_type=F32) * switch[:, None]
    count = w_gate.shape[0]
    mine = position * count + jnp.arange(count, dtype=jnp.int32)
    shares = jnp.sum(
        jnp.where(route_ids[:, :, None] == mine, route_weights[:, :, None], 0.0), axis=1
    )
    shares = jnp.roll(shares.T.reshape(count, SIDE, SIDE, 2, tok_dev // 2), (-y, -x), (1, 2))
    share_first = jnp.transpose(shares[:, :, :, 0], (1, 2, 3, 0))
    share_second = jnp.transpose(shares[:, :, :, 1], (2, 1, 3, 0))
    made = {}
    previous = None
    for k in (0, 1, 2, 3):
        xa, xb = firsts[k], seconds[k]
        if previous is not None:
            xa, xb, *made[previous] = lax.optimization_barrier((xa, xb, *made[previous]))
        made[k] = expert_mix(xa, xb, share_first[k], share_second[k], w_gate, w_up, w_down)
        previous = k
    routed = scatter_sums(lambda k: made[k % SIDE][0], lambda k: made[k % SIDE][1])
    return (residual + shared + routed).astype(BF16)


def solution(mesh):
    in_specs = (
        P(("seq", "exp"), None),
        P(),
        P(None, "exp"),
        P(None, "exp"),
        P(None, "exp"),
        P(None, "exp"),
        P("exp", "seq"),
        P("exp", "seq"),
        P(),
        P("exp", None),
        P(),
        P("seq", None),
        P("seq", None),
        P("exp", None, None),
        P("exp", None, None),
        P("exp", None, None),
        P(),
        P(),
        P(),
        P(),
    )
    out_specs = P(("seq", "exp"), None)
    return jax.shard_map(local, mesh=mesh, in_specs=in_specs, out_specs=out_specs, check_vma=False)
```

```python
import jax
import jax.numpy as jnp
from jax import lax
from jax.experimental import pallas as pl
from jax.experimental.pallas import tpu as pltpu
from jax.sharding import PartitionSpec as P

DK = 128
DV = 128
BLOCK = 128
F32 = jnp.float32
BF16 = jnp.bfloat16
NN = (((1,), (0,)), ((), ()))
NT = (((1,), (1,)), ((), ()))
TN = (((0,), (0,)), ((), ()))


def row_norm(values, gain_vec, epsilon):
    return (
        values * lax.rsqrt(jnp.mean(values * values, axis=-1, keepdims=True) + epsilon) * gain_vec
    )


def split(x):
    hi = x.astype(BF16)
    return hi, (x - hi.astype(F32)).astype(BF16)


def mm(a, b, dims=NN):
    return lax.dot_general(a, b, dims, preferred_element_type=F32)


def dot3_narrow(a, b):
    ah, al = split(a)
    bh, bl = split(b)
    left = jnp.concatenate([ah, al], axis=1)
    right = jnp.concatenate(
        [jnp.concatenate([bh, bl], axis=1), jnp.concatenate([bh, jnp.zeros_like(bl)], axis=1)],
        axis=0,
    )
    both = mm(left, right)
    return both[:, :128] + both[:, 128:]


def dot3_wide(a, b):
    ah, al = split(a)
    bh, bl = split(b)
    return mm(jnp.concatenate([ah, al], axis=1), jnp.concatenate([bh, bh], axis=0)) + mm(ah, bl)


def delta_kernel(blocks, place_ref, *refs):
    proj_refs, (cum_ref, rate_ref, base_ref, reach_ref, total_ref, state) = refs[:-6], refs[-6:]
    step = pl.program_id(0)
    rows = lax.broadcasted_iota(jnp.int32, (BLOCK, BLOCK), 0)
    cols = lax.broadcasted_iota(jnp.int32, (BLOCK, BLOCK), 1)
    causal = rows >= cols
    strict = rows > cols
    apart = rows ^ cols
    eye = jnp.where(rows == cols, 1.0, 0.0).astype(F32)
    heads = 2

    @pl.when(step == 0)
    def _():
        for h in range(heads):
            state[h] = jnp.concatenate([eye, jnp.zeros((DK, DV), F32)], axis=1)

    problems = []
    for b in range(blocks):
        first_ref, second_ref = proj_refs[2 * (b // SIDE) : 2 * (b // SIDE) + 2]
        away = lax.rem(b % SIDE - place_ref[1] + SIDE, SIDE)

        def columns(start, size, first_ref=first_ref, second_ref=second_ref, away=away):
            return jnp.concatenate(
                [first_ref[0, away, :, start : start + size], second_ref[away, 0, :, start : start + size]],
                axis=0,
            )

        query = columns(0, DK)
        key = columns(DK, DK)
        key = key * lax.rsqrt(jnp.sum(key * key, axis=-1, keepdims=True) + 1e-06)
        qh, ql = split(query)
        kh, kl = split(key)
        stacked_h = jnp.concatenate([kh, qh], axis=0)
        stacked_l = jnp.concatenate([kl, ql], axis=0)
        products = mm(stacked_h, kh, NT) + (mm(stacked_h, kl, NT) + mm(stacked_l, kh, NT))
        key_key, query_key = products[:BLOCK], products[BLOCK:]
        for h in range(heads):
            cum_row = jnp.broadcast_to(cum_ref[h, b : b + 1, :], (BLOCK, BLOCK))
            rate_row = jnp.broadcast_to(rate_ref[h, b : b + 1, :], (BLOCK, BLOCK))
            cum_col = cum_row.T
            rate_col = rate_row.T
            ratios = jnp.where(causal, jnp.exp(jnp.where(causal, cum_col - cum_row, 0.0)), 0.0)
            weighted = ratios * rate_row
            lower = jnp.where(strict, weighted * key_key, 0.0)
            mixing = weighted * query_key
            decays = jnp.exp(cum_col)
            last = cum_col[BLOCK - 1 : BLOCK, :]
            key_tail = key * (jnp.exp(last - cum_col) * rate_col)
            value = columns(2 * DK + h * DV, DV)
            problems.append(
                dict(
                    b=b,
                    h=h,
                    lower=lower,
                    mixing=mixing,
                    right=jnp.concatenate([value, decays * key], axis=1),
                    query=decays * query,
                    key_tail=key_tail,
                    fade=jnp.exp(last) * eye,
                    inverse=eye - jnp.where(apart == 1, lower, 0.0),
                )
            )
    size = 2
    while size < BLOCK:
        for p in problems:
            part = jnp.where((apart >= size) & (apart < 2 * size), p["lower"], 0.0)
            p["inner"] = dot3_narrow(part, p["inverse"])
        for p in problems:
            p["inverse"] = p["inverse"] - dot3_narrow(p["inverse"], p["inner"])
        size *= 2
    for p in problems:
        p["solved"] = dot3_wide(p["inverse"], p["right"])
    for p in problems:
        p["mixed"] = dot3_wide(p["mixing"], p["solved"])
        p["tail"] = dot3_wide(p["key_tail"].T, p["solved"])
    for p in problems:
        h = p["h"]
        span = slice(p["b"] * BLOCK, (p["b"] + 1) * BLOCK)
        cols_h = slice(h * DV, (h + 1) * DV)
        before = state[h]
        effective = p["query"] - p["mixed"][:, DV:]
        seen = dot3_wide(effective, before)
        reach_ref[span, cols_h] = seen[:, :DK]
        base_ref[span, cols_h] = p["mixed"][:, :DV] + seen[:, DK:]
        moved = dot3_wide(p["fade"] - p["tail"][:, DV:], before)
        state[h] = jnp.concatenate([moved[:, :DK], moved[:, DK:] + p["tail"][:, :DV]], axis=1)

    @pl.when(step == pl.num_programs(0) - 1)
    def _():
        total_ref[...] = state[...]


def away_of(row, place, which):
    return lax.rem(row - place[which] + SIDE, SIDE)


def delta_local(place, first, second, cumulative, rates):
    _, _, part, columns = first.shape
    tokens = 2 * SIDE * SIDE * part
    rows = 2
    blocks = rows * SIDE
    specs = []
    for r in range(rows):
        specs += [
            pl.BlockSpec(
                (1, SIDE, part, columns), lambda i, p, r=r: (away_of(rows * i + r, p, 0), 0, 0, 0)
            ),
            pl.BlockSpec(
                (SIDE, 1, part, columns), lambda i, p, r=r: (0, away_of(rows * i + r, p, 0), 0, 0)
            ),
        ]
    return pl.pallas_call(
        lambda *refs: delta_kernel(blocks, *refs),
        grid_spec=pltpu.PrefetchScalarGridSpec(
            num_scalar_prefetch=1,
            grid=(SIDE // rows,),
            in_specs=specs
            + [
                pl.BlockSpec((2, blocks, BLOCK), lambda i, p: (0, i, 0)),
                pl.BlockSpec((2, blocks, BLOCK), lambda i, p: (0, i, 0)),
            ],
            out_specs=[
                pl.BlockSpec((blocks * BLOCK, 2 * DV), lambda i, p: (i, 0)),
                pl.BlockSpec((blocks * BLOCK, 2 * DV), lambda i, p: (i, 0)),
                pl.BlockSpec((2, DK, DK + DV), lambda i, p: (0, 0, 0)),
            ],
            scratch_shapes=[pltpu.VMEM((2, DK, DK + DV), F32)],
        ),
        out_shape=[
            jax.ShapeDtypeStruct((tokens, 2 * DV), F32),
            jax.ShapeDtypeStruct((tokens, 2 * DV), F32),
            jax.ShapeDtypeStruct((2, DK, DK + DV), F32),
        ],
        compiler_params=pltpu.CompilerParams(vmem_limit_bytes=60 * 2**20),
        cost_estimate=pl.CostEstimate(flops=2 * 10**10, bytes_accessed=10**7, transcendentals=0),
        name="delta_local",
    )(place, *([first, second] * rows), cumulative, rates)


def gate_kernel(
    place_ref, maps_ref, base_ref, reach_ref, first_ref, second_ref, gain_ref, out_ref, entering
):
    @pl.when(pl.program_id(0) == 0)
    def _():
        states = [jnp.zeros((DK, DV), F32)] * 2
        for j in range(maps_ref.shape[0]):
            for h in range(2):
                pair = maps_ref[j, h]
                high, low = split(states[h])
                moved = mm(pair[:, :DK], jnp.concatenate([high, low], axis=1))
                states[h] = moved[:, :DV] + moved[:, DV:] + pair[:, DK:].astype(F32)
                if j == maps_ref.shape[0] - 2:
                    entering[h] = states[h]
        for h in range(2):
            entering[h] = jnp.where(place_ref[2] == 1, states[h], entering[h])

    rows = base_ref.shape[0] // SIDE
    for h in range(2):
        span = slice(h * DV, (h + 1) * DV)
        attended = base_ref[:, span] + dot3_narrow(reach_ref[:, span], entering[h])
        scaled = row_norm(attended, gain_ref[...], 1e-06)
        for x in range(SIDE):
            away = lax.rem(x - place_ref[1] + SIDE, SIDE)
            u = jnp.concatenate([first_ref[0, away, :, span], second_ref[away, 0, :, span]], axis=0)
            here = slice(x * rows, (x + 1) * rows)
            out_ref[here, span] = (scaled[here] * (u / (1.0 + jnp.exp(-u)))).astype(out_ref.dtype)


def delta_gate(place, maps, base, reach, first, second, gain):
    tokens = base.shape[0]
    rows = tokens // SIDE
    part = first.shape[2]
    return pl.pallas_call(
        gate_kernel,
        grid_spec=pltpu.PrefetchScalarGridSpec(
            num_scalar_prefetch=1,
            grid=(SIDE,),
            in_specs=[
                pl.BlockSpec(maps.shape, lambda i, p: (0, 0, 0, 0)),
                pl.BlockSpec((rows, 2 * DV), lambda i, p: (i, 0)),
                pl.BlockSpec((rows, 2 * DV), lambda i, p: (i, 0)),
                pl.BlockSpec((1, SIDE, part, 2 * DV), lambda i, p: (away_of(i, p, 0), 0, 0, 2)),
                pl.BlockSpec((SIDE, 1, part, 2 * DV), lambda i, p: (0, away_of(i, p, 0), 0, 2)),
                pl.BlockSpec((1, DV), lambda i, p: (0, 0)),
            ],
            out_specs=pl.BlockSpec((rows, 2 * DV), lambda i, p: (i, 0)),
            scratch_shapes=[pltpu.VMEM((2, DK, DV), F32)],
        ),
        out_shape=jax.ShapeDtypeStruct((tokens, 2 * DV), BF16),
        compiler_params=pltpu.CompilerParams(vmem_limit_bytes=60 * 2**20),
        cost_estimate=pl.CostEstimate(flops=10**9, bytes_accessed=10**7, transcendentals=10**6),
        name="delta_gate",
    )(place, maps, base, reach, first, second, gain)


def expert_kernel(xa_ref, xb_ref, sa_ref, sb_ref, gate_ref, up_ref, down_ref, oa_ref, ob_ref, x_ref, total):
    width = xa_ref.shape[-1]
    rows = xa_ref.size // width
    step = pl.program_id(0)
    expert = step // EXPERT_CUTS

    @pl.when(step == 0)
    def _():
        x_ref[:rows] = xa_ref[...].reshape(rows, width)
        x_ref[rows:] = xb_ref[...].reshape(rows, width)

    x = x_ref[...]
    shares = jnp.concatenate(
        [sa_ref[...].reshape(rows, -1), sb_ref[...].reshape(rows, -1)], axis=0
    )
    share = jnp.where(expert == 0, shares[:, 0:1], shares[:, 1:2])
    gated = mm(x, gate_ref[0])
    raised = mm(x, up_ref[0])
    hidden = gated / (1.0 + jnp.exp(-gated)) * raised * share
    made = mm(hidden.astype(BF16), down_ref[0])

    @pl.when(step == 0)
    def _():
        total[...] = made

    @pl.when((step > 0) & (step < pl.num_programs(0) - 1))
    def _():
        total[...] += made

    @pl.when(step == pl.num_programs(0) - 1)
    def _():
        done = (total[...] + made).astype(oa_ref.dtype)
        oa_ref[...] = done[:rows].reshape(oa_ref.shape)
        ob_ref[...] = done[rows:].reshape(ob_ref.shape)


EXPERT_CUTS = 2


def expert_mix(xa, xb, sa, sb, w_gate, w_up, w_down):
    side, part, width = xa.shape
    count, _, inner = w_gate.shape
    cut = inner // EXPERT_CUTS
    whole = lambda i: (0, 0, 0)
    rows_spec = pl.BlockSpec((side, part, width), whole, pipeline_mode=pl.Buffered(1))
    share_spec = pl.BlockSpec((side, part, count), whole, pipeline_mode=pl.Buffered(1))
    out_spec = pl.BlockSpec((side, part, width), whole)
    across = pl.BlockSpec((1, width, cut), lambda i: (i // EXPERT_CUTS, 0, i % EXPERT_CUTS))
    down = pl.BlockSpec((1, cut, width), lambda i: (i // EXPERT_CUTS, i % EXPERT_CUTS, 0))
    return pl.pallas_call(
        expert_kernel,
        grid=(count * EXPERT_CUTS,),
        in_specs=[rows_spec, rows_spec, share_spec, share_spec, across, across, down],
        out_specs=[out_spec, out_spec],
        out_shape=[jax.ShapeDtypeStruct((side, part, width), BF16)] * 2,
        scratch_shapes=[
            pltpu.VMEM((2 * side * part, width), BF16),
            pltpu.VMEM((2 * side * part, width), F32),
        ],
        compiler_params=pltpu.CompilerParams(vmem_limit_bytes=48 * 2**20),
        cost_estimate=pl.CostEstimate(
            flops=12 * side * part * count * width * inner,
            bytes_accessed=6 * count * width * inner + 8 * side * part * width,
            transcendentals=2 * side * part * count * inner,
        ),
        name="expert_mix",
    )(xa, xb, sa, sb, w_gate, w_up, w_down)


SIDE = 4


def neighbour(value, axis, by):
    pairs = []
    for y in range(SIDE):
        for x in range(SIDE):
            ny, nx = ((y + by) % SIDE, x) if axis == 0 else (y, (x + by) % SIDE)
            pairs.append((y * SIDE + x, ny * SIDE + nx))
    return lax.ppermute(value, "exp", pairs)


def plus(*terms):
    total = terms[0].astype(F32)
    for term in terms[1:]:
        total = total + term.astype(F32)
    return total


def reduce_ring(groups, axis, final):
    far = groups(2)
    half = far.shape[0] // 2
    up = neighbour(far[:half], axis, 1)
    down = neighbour(far[half:], axis, -1)
    ahead, behind = groups(1), groups(-1)
    ahead = jnp.concatenate([plus(ahead[:half], up).astype(BF16), ahead[half:]], axis=0)
    behind = jnp.concatenate([behind[:half], plus(behind[half:], down).astype(BF16)], axis=0)
    from_behind = neighbour(ahead, axis, 1)
    from_ahead = neighbour(behind, axis, -1)
    return plus(groups(0), from_behind, from_ahead).astype(final)


def scatter_sums(first, second):
    a = reduce_ring(first, 0, BF16)
    b = reduce_ring(second, 1, BF16)
    a = reduce_ring(lambda k: a[k % SIDE], 1, F32)
    b = reduce_ring(lambda k: b[k % SIDE], 0, F32)
    return jnp.concatenate([a, b], axis=0)


def gather_direct(block, axis):
    return [
        block,
        neighbour(block, axis, -1),
        neighbour(block, axis, 2),
        neighbour(block, axis, 1),
    ]


def gather_rows(rows, tied):
    tie = lax.optimization_barrier if tied else (lambda v: v)
    part = rows.shape[0] // 2
    a, b = gather_direct(rows[:part], 1), gather_direct(rows[part:], 0)
    a, b = tie((a, b))
    a, b = jnp.stack(a), jnp.stack(b)
    half = a.shape[0] // 2
    a_behind, a_ahead = neighbour(a, 0, 1), neighbour(a, 0, -1)
    b_behind, b_ahead = neighbour(b, 1, 1), neighbour(b, 1, -1)
    a_behind, a_ahead, b_behind, b_ahead = tie((a_behind, a_ahead, b_behind, b_ahead))
    a_far = (neighbour(a_behind[:half], 0, 1), neighbour(a_ahead[half:], 0, -1))
    b_far = (neighbour(b_behind[:half], 1, 1), neighbour(b_ahead[half:], 1, -1))
    first = [a, a_ahead, jnp.concatenate(a_far, axis=0), a_behind]
    second = [b, b_ahead, jnp.concatenate(b_far, axis=0), b_behind]
    return first, second


def along_seq(value, pairs):
    return lax.ppermute(value, "seq", pairs)


def other_core(value):
    return along_seq(value, [(i, i ^ 1) for i in range(lax.axis_size("seq"))])


def relay(total, core):
    mine = total.astype(BF16)
    theirs = other_core(mine)
    early = jnp.where(core == 0, mine, theirs)
    late = jnp.where(core == 0, theirs, mine)
    chip = jnp.einsum("hkl,hlm->hkm", late[:, :, :DK], early, preferred_element_type=F32)
    chip = jnp.concatenate([chip[:, :, :DK], chip[:, :, DK:] + late[:, :, DK:].astype(F32)], axis=2)
    chip = chip.astype(BF16)
    size = lax.axis_size("seq")
    shifts = [along_seq(chip, [(i, i + 2 * d) for i in range(size - 2 * d)]) for d in (3, 2, 1)]
    return jnp.stack(shifts + [theirs])


def local(
    tokens,
    norm_in,
    w_query,
    w_key,
    w_value,
    w_outgate,
    log_decay,
    write_rate,
    head_gain,
    w_output,
    norm_post,
    route_ids,
    route_weights,
    w_gate,
    w_up,
    w_down,
    w_shared_gate,
    w_shared_up,
    w_shared_down,
    w_shared_switch,
):
    tok_dev = tokens.shape[0]
    owners = lax.axis_size("exp")
    tok_seq = tok_dev * owners
    position = lax.axis_index("exp")
    residual_in = tokens.astype(F32)
    normed = row_norm(residual_in, norm_in, 1e-06).astype(BF16)
    w_all = jnp.concatenate([w_query, w_key, w_value, w_outgate], axis=1)
    y, x = position // SIDE, position % SIDE
    core = lax.axis_index("seq") % 2
    place = jnp.stack([y, x, core]).astype(jnp.int32)
    firsts, seconds = gather_rows(normed, True)

    def project(rows):
        made = jnp.dot(rows.reshape(-1, rows.shape[-1]), w_all, preferred_element_type=F32)
        return made.reshape(rows.shape[0], rows.shape[1], -1)

    firsts = [project(v) for v in firsts]
    seconds = [project(v) for v in seconds]
    half = w_output.shape[1] // 2
    w_half = lax.dynamic_slice_in_dim(w_output, core * half, half, 1)
    w_half, firsts, seconds = lax.optimization_barrier((w_half, firsts, seconds))
    first, second = jnp.stack(firsts), jnp.stack(seconds)
    w_half = lax.all_gather(w_half, "exp", axis=0)
    blocks = tok_seq // BLOCK
    cumulative = jnp.cumsum(log_decay.reshape(2, blocks, BLOCK), axis=-1)
    base, reach, total = delta_local(
        place, first, second, cumulative, write_rate.reshape(2, blocks, BLOCK)
    )
    maps = relay(total, core)
    gated = delta_gate(place, maps, base, reach, first, second, head_gain.reshape(1, DV))
    arrived = lax.all_to_all(
        gated.reshape(owners, tok_dev, -1), "exp", split_axis=0, concat_axis=0, tiled=True
    )
    theirs = other_core(arrived)
    mix = lambda rows: jnp.einsum("stc,scd->td", rows, w_half, preferred_element_type=F32)
    back = other_core(mix(theirs).astype(BF16)).astype(F32)
    kept = mix(arrived)
    mixed_out = jnp.concatenate(
        [jnp.where(core == 0, kept, back), jnp.where(core == 0, back, kept)], axis=1
    )
    residual = residual_in + mixed_out
    post_norm = row_norm(residual, norm_post, 1e-06).astype(BF16)
    rows_first, rows_second = gather_rows(post_norm, False)
    switch = jax.nn.sigmoid(jnp.dot(post_norm, w_shared_switch, preferred_element_type=F32))
    inner_act = (
        jax.nn.silu(jnp.dot(post_norm, w_shared_gate, preferred_element_type=F32))
        * jnp.dot(post_norm, w_shared_up, preferred_element_type=F32)
    ).astype(BF16)
    shared = jnp.dot(inner_act, w_shared_down, preferred_element_type=F32) * switch[:, None]
    count = w_gate.shape[0]
    mine = position * count + jnp.arange(count, dtype=jnp.int32)
    shares = jnp.sum(
        jnp.where(route_ids[:, :, None] == mine, route_weights[:, :, None], 0.0), axis=1
    )
    shares = jnp.roll(shares.T.reshape(count, SIDE, SIDE, 2, tok_dev // 2), (-y, -x), (1, 2))
    share_first = jnp.transpose(shares[:, :, :, 0], (1, 2, 3, 0))
    share_second = jnp.transpose(shares[:, :, :, 1], (2, 1, 3, 0))
    made = {}
    previous = None
    for k in (0, 1, 2, 3):
        xa, xb = rows_first[k], rows_second[k]
        if previous is None:
            xa, xb, shared = lax.optimization_barrier((xa, xb, shared))
        else:
            xa, xb, *made[previous] = lax.optimization_barrier((xa, xb, *made[previous]))
        made[k] = expert_mix(xa, xb, share_first[k], share_second[k], w_gate, w_up, w_down)
        previous = k
    routed = scatter_sums(lambda k: made[k % SIDE][0], lambda k: made[k % SIDE][1])
    return (residual + shared + routed).astype(BF16)


def solution(mesh):
    in_specs = (
        P(("seq", "exp"), None),
        P(),
        P(None, "exp"),
        P(None, "exp"),
        P(None, "exp"),
        P(None, "exp"),
        P("exp", "seq"),
        P("exp", "seq"),
        P(),
        P("exp", None),
        P(),
        P("seq", None),
        P("seq", None),
        P("exp", None, None),
        P("exp", None, None),
        P("exp", None, None),
        P(),
        P(),
        P(),
        P(),
    )
    out_specs = P(("seq", "exp"), None)
    return jax.shard_map(local, mesh=mesh, in_specs=in_specs, out_specs=out_specs, check_vma=False)
```

```python
import jax
import jax.numpy as jnp
from jax import lax
from jax.experimental import pallas as pl
from jax.experimental.pallas import tpu as pltpu
from jax.sharding import PartitionSpec as P

DK = 128
DV = 128
BLOCK = 128
F32 = jnp.float32
BF16 = jnp.bfloat16
NN = (((1,), (0,)), ((), ()))
NT = (((1,), (1,)), ((), ()))
TN = (((0,), (0,)), ((), ()))


def row_norm(values, gain_vec, epsilon):
    return (
        values * lax.rsqrt(jnp.mean(values * values, axis=-1, keepdims=True) + epsilon) * gain_vec
    )


def split(x):
    hi = x.astype(BF16)
    return hi, (x - hi.astype(F32)).astype(BF16)


def mm(a, b, dims=NN):
    return lax.dot_general(a, b, dims, preferred_element_type=F32)


def dot3_narrow(a, b):
    ah, al = split(a)
    bh, bl = split(b)
    left = jnp.concatenate([ah, al], axis=1)
    right = jnp.concatenate(
        [jnp.concatenate([bh, bl], axis=1), jnp.concatenate([bh, jnp.zeros_like(bl)], axis=1)],
        axis=0,
    )
    both = mm(left, right)
    return both[:, :128] + both[:, 128:]


def dot3_wide(a, b):
    ah, al = split(a)
    bh, bl = split(b)
    return mm(jnp.concatenate([ah, al], axis=1), jnp.concatenate([bh, bh], axis=0)) + mm(ah, bl)


def delta_kernel(
    blocks,
    place_ref,
    *refs,
):
    gathered, refs = refs[: 2 * SIDE], refs[2 * SIDE :]
    query_ref, key_ref, value_ref, outgate_ref, cum_ref, rate_ref = refs[:6]
    base_ref, reach_ref, gate_ref, total_ref, state, held, lines, proj_ref, arrived = refs[6:]
    step = pl.program_id(0)

    @pl.when(step == 0)
    def _():
        copies = [
            pltpu.make_async_copy(ref, held.at[i // SIDE, i % SIDE], arrived.at[i])
            for i, ref in enumerate(gathered)
        ]
        for copy in copies:
            copy.start()
        for copy in copies:
            copy.wait()

    part = held.shape[3]
    pair = 2

    def project(c, carry):
        for u in range(pair):
            block = c * pair + u
            far_y = lax.rem(step * (blocks // SIDE) + block // SIDE - place_ref[0] + SIDE, SIDE)
            far_x = lax.rem(block % SIDE - place_ref[1] + SIDE, SIDE)
            lines[u * BLOCK : u * BLOCK + part] = held[0, far_y, far_x]
            lines[u * BLOCK + part : (u + 1) * BLOCK] = held[1, far_x, far_y]
        x = lines[...]
        span = pl.ds(pl.multiple_of(c * pair * BLOCK, pair * BLOCK), pair * BLOCK)
        proj_ref[span, 0:DK] = mm(x, query_ref[...])
        proj_ref[span, DK : 2 * DK] = mm(x, key_ref[...])
        proj_ref[span, 2 * DK :] = mm(x, value_ref[...])
        gate_ref[span, :] = mm(x, outgate_ref[...])
        return carry

    lax.fori_loop(0, blocks // pair, project, 0)
    rows = lax.broadcasted_iota(jnp.int32, (BLOCK, BLOCK), 0)
    cols = lax.broadcasted_iota(jnp.int32, (BLOCK, BLOCK), 1)
    causal = rows >= cols
    strict = rows > cols
    apart = rows ^ cols
    eye = jnp.where(rows == cols, 1.0, 0.0).astype(F32)
    heads = 2

    @pl.when(step == 0)
    def _():
        for h in range(heads):
            state[h] = jnp.concatenate([eye, jnp.zeros((DK, DV), F32)], axis=1)

    problems = []
    for b in range(blocks):
        span = slice(b * BLOCK, (b + 1) * BLOCK)
        query = proj_ref[span, 0:DK]
        key = proj_ref[span, DK : 2 * DK]
        key = key * lax.rsqrt(jnp.sum(key * key, axis=-1, keepdims=True) + 1e-06)
        qh, ql = split(query)
        kh, kl = split(key)
        stacked_h = jnp.concatenate([kh, qh], axis=0)
        stacked_l = jnp.concatenate([kl, ql], axis=0)
        products = mm(stacked_h, kh, NT) + (mm(stacked_h, kl, NT) + mm(stacked_l, kh, NT))
        key_key, query_key = products[:BLOCK], products[BLOCK:]
        for h in range(heads):
            cum_row = jnp.broadcast_to(cum_ref[h, b : b + 1, :], (BLOCK, BLOCK))
            rate_row = jnp.broadcast_to(rate_ref[h, b : b + 1, :], (BLOCK, BLOCK))
            cum_col = cum_row.T
            rate_col = rate_row.T
            ratios = jnp.where(causal, jnp.exp(jnp.where(causal, cum_col - cum_row, 0.0)), 0.0)
            weighted = ratios * rate_row
            lower = jnp.where(strict, weighted * key_key, 0.0)
            mixing = weighted * query_key
            decays = jnp.exp(cum_col)
            last = cum_col[BLOCK - 1 : BLOCK, :]
            key_tail = key * (jnp.exp(last - cum_col) * rate_col)
            value = proj_ref[span, 2 * DK + h * DV : 2 * DK + (h + 1) * DV]
            problems.append(
                dict(
                    b=b,
                    h=h,
                    lower=lower,
                    mixing=mixing,
                    right=jnp.concatenate([value, decays * key], axis=1),
                    query=decays * query,
                    key_tail=key_tail,
                    fade=jnp.exp(last) * eye,
                    inverse=eye - jnp.where(apart == 1, lower, 0.0),
                )
            )
    size = 2
    while size < BLOCK:
        for p in problems:
            part = jnp.where((apart >= size) & (apart < 2 * size), p["lower"], 0.0)
            p["inner"] = dot3_narrow(part, p["inverse"])
        for p in problems:
            p["inverse"] = p["inverse"] - dot3_narrow(p["inverse"], p["inner"])
        size *= 2
    for p in problems:
        p["solved"] = dot3_wide(p["inverse"], p["right"])
    for p in problems:
        p["mixed"] = dot3_wide(p["mixing"], p["solved"])
        p["tail"] = dot3_wide(p["key_tail"].T, p["solved"])
    for p in problems:
        h = p["h"]
        span = slice(p["b"] * BLOCK, (p["b"] + 1) * BLOCK)
        cols_h = slice(h * DV, (h + 1) * DV)
        before = state[h]
        effective = p["query"] - p["mixed"][:, DV:]
        seen = dot3_wide(effective, before)
        reach_ref[span, cols_h] = seen[:, :DK]
        base_ref[span, cols_h] = p["mixed"][:, :DV] + seen[:, DK:]
        moved = dot3_wide(p["fade"] - p["tail"][:, DV:], before)
        state[h] = jnp.concatenate([moved[:, :DK], moved[:, DK:] + p["tail"][:, :DV]], axis=1)

    @pl.when(step == pl.num_programs(0) - 1)
    def _():
        total_ref[...] = state[...]


def delta_local(place, firsts, seconds, weights, cumulative, rates):
    side, part, width = firsts[0].shape
    tokens = 2 * side * side * part
    blocks = 8
    whole = lambda i, p: (0, 0)
    lines = pl.BlockSpec((blocks * BLOCK, 2 * DV), lambda i, p: (i, 0))
    rates_spec = pl.BlockSpec((2, blocks, BLOCK), lambda i, p: (0, i, 0))
    return pl.pallas_call(
        lambda *refs: delta_kernel(blocks, *refs),
        grid_spec=pltpu.PrefetchScalarGridSpec(
            num_scalar_prefetch=1,
            grid=(tokens // (blocks * BLOCK),),
            in_specs=[pl.BlockSpec(memory_space=pl.ANY)] * (2 * side)
            + [pl.BlockSpec(w.shape, whole, pipeline_mode=pl.Buffered(1)) for w in weights]
            + [rates_spec, rates_spec],
            out_specs=[
                lines,
                lines,
                lines,
                pl.BlockSpec((2, DK, DK + DV), lambda i, p: (0, 0, 0)),
            ],
            scratch_shapes=[
                pltpu.VMEM((2, DK, DK + DV), F32),
                pltpu.VMEM((2, side, side, part, width), BF16),
                pltpu.VMEM((2 * BLOCK, width), BF16),
                pltpu.VMEM((blocks * BLOCK, 2 * DK + 2 * DV), F32),
                pltpu.SemaphoreType.DMA((2 * side,)),
            ],
        ),
        out_shape=[jax.ShapeDtypeStruct((tokens, 2 * DV), F32)] * 3
        + [jax.ShapeDtypeStruct((2, DK, DK + DV), F32)],
        compiler_params=pltpu.CompilerParams(vmem_limit_bytes=60 * 2**20),
        cost_estimate=pl.CostEstimate(
            flops=3 * 10**10, bytes_accessed=2 * 10**7, transcendentals=0
        ),
        name="delta_local",
    )(place, *firsts, *seconds, *weights, cumulative, rates)


def gate_kernel(
    place_ref, maps_ref, base_ref, reach_ref, gate_ref, gain_ref, out_ref, entering
):
    @pl.when(pl.program_id(0) == 0)
    def _():
        states = [jnp.zeros((DK, DV), F32)] * 2
        for j in range(maps_ref.shape[0]):
            for h in range(2):
                pair = maps_ref[j, h]
                high, low = split(states[h])
                moved = mm(pair[:, :DK], jnp.concatenate([high, low], axis=1))
                states[h] = moved[:, :DV] + moved[:, DV:] + pair[:, DK:].astype(F32)
                if j == maps_ref.shape[0] - 2:
                    entering[h] = states[h]
        for h in range(2):
            entering[h] = jnp.where(place_ref[2] == 1, states[h], entering[h])

    for h in range(2):
        span = slice(h * DV, (h + 1) * DV)
        attended = base_ref[:, span] + dot3_narrow(reach_ref[:, span], entering[h])
        scaled = row_norm(attended, gain_ref[...], 1e-06)
        u = gate_ref[:, span]
        out_ref[:, span] = (scaled * (u / (1.0 + jnp.exp(-u)))).astype(out_ref.dtype)


def delta_gate(place, maps, base, reach, gate, gain):
    tokens = base.shape[0]
    rows = 512
    lines = pl.BlockSpec((rows, 2 * DV), lambda i, p: (i, 0))
    return pl.pallas_call(
        gate_kernel,
        grid_spec=pltpu.PrefetchScalarGridSpec(
            num_scalar_prefetch=1,
            grid=(tokens // rows,),
            in_specs=[
                pl.BlockSpec(maps.shape, lambda i, p: (0, 0, 0, 0)),
                lines,
                lines,
                lines,
                pl.BlockSpec((1, DV), lambda i, p: (0, 0)),
            ],
            out_specs=lines,
            scratch_shapes=[pltpu.VMEM((2, DK, DV), F32)],
        ),
        out_shape=jax.ShapeDtypeStruct((tokens, 2 * DV), BF16),
        compiler_params=pltpu.CompilerParams(vmem_limit_bytes=60 * 2**20),
        cost_estimate=pl.CostEstimate(flops=10**9, bytes_accessed=10**7, transcendentals=10**6),
        name="delta_gate",
    )(place, maps, base, reach, gate, gain)


def expert_kernel(xa_ref, xb_ref, sa_ref, sb_ref, gate_ref, up_ref, down_ref, oa_ref, ob_ref, x_ref, total):
    width = xa_ref.shape[-1]
    rows = xa_ref.size // width
    step = pl.program_id(0)
    expert = step // EXPERT_CUTS

    @pl.when(step == 0)
    def _():
        x_ref[:rows] = xa_ref[...].reshape(rows, width)
        x_ref[rows:] = xb_ref[...].reshape(rows, width)

    x = x_ref[...]
    shares = jnp.concatenate(
        [sa_ref[...].reshape(rows, -1), sb_ref[...].reshape(rows, -1)], axis=0
    )
    share = jnp.where(expert == 0, shares[:, 0:1], shares[:, 1:2])
    gated = mm(x, gate_ref[0])
    raised = mm(x, up_ref[0])
    hidden = gated / (1.0 + jnp.exp(-gated)) * raised * share
    made = mm(hidden.astype(BF16), down_ref[0])

    @pl.when(step == 0)
    def _():
        total[...] = made

    @pl.when((step > 0) & (step < pl.num_programs(0) - 1))
    def _():
        total[...] += made

    @pl.when(step == pl.num_programs(0) - 1)
    def _():
        done = (total[...] + made).astype(oa_ref.dtype)
        oa_ref[...] = done[:rows].reshape(oa_ref.shape)
        ob_ref[...] = done[rows:].reshape(ob_ref.shape)


EXPERT_CUTS = 2


def expert_mix(xa, xb, sa, sb, w_gate, w_up, w_down):
    side, part, width = xa.shape
    count, _, inner = w_gate.shape
    cut = inner // EXPERT_CUTS
    whole = lambda i: (0, 0, 0)
    rows_spec = pl.BlockSpec((side, part, width), whole, pipeline_mode=pl.Buffered(1))
    share_spec = pl.BlockSpec((side, part, count), whole, pipeline_mode=pl.Buffered(1))
    out_spec = pl.BlockSpec((side, part, width), whole)
    across = pl.BlockSpec((1, width, cut), lambda i: (i // EXPERT_CUTS, 0, i % EXPERT_CUTS))
    down = pl.BlockSpec((1, cut, width), lambda i: (i // EXPERT_CUTS, i % EXPERT_CUTS, 0))
    return pl.pallas_call(
        expert_kernel,
        grid=(count * EXPERT_CUTS,),
        in_specs=[rows_spec, rows_spec, share_spec, share_spec, across, across, down],
        out_specs=[out_spec, out_spec],
        out_shape=[jax.ShapeDtypeStruct((side, part, width), BF16)] * 2,
        scratch_shapes=[
            pltpu.VMEM((2 * side * part, width), BF16),
            pltpu.VMEM((2 * side * part, width), F32),
        ],
        compiler_params=pltpu.CompilerParams(vmem_limit_bytes=48 * 2**20),
        cost_estimate=pl.CostEstimate(
            flops=12 * side * part * count * width * inner,
            bytes_accessed=6 * count * width * inner + 8 * side * part * width,
            transcendentals=2 * side * part * count * inner,
        ),
        name="expert_mix",
    )(xa, xb, sa, sb, w_gate, w_up, w_down)


SIDE = 4


def neighbour(value, axis, by):
    pairs = []
    for y in range(SIDE):
        for x in range(SIDE):
            ny, nx = ((y + by) % SIDE, x) if axis == 0 else (y, (x + by) % SIDE)
            pairs.append((y * SIDE + x, ny * SIDE + nx))
    return lax.ppermute(value, "exp", pairs)


def plus(*terms):
    total = terms[0].astype(F32)
    for term in terms[1:]:
        total = total + term.astype(F32)
    return total


def far_sums(groups, axis):
    far = groups(2)
    half = far.shape[0] // 2
    return neighbour(far[:half], axis, 1), neighbour(far[half:], axis, -1)


def near_sums(groups, axis, up, down, final):
    half = up.shape[0]
    ahead, behind = groups(1), groups(-1)
    ahead = jnp.concatenate([plus(ahead[:half], up).astype(BF16), ahead[half:]], axis=0)
    behind = jnp.concatenate([behind[:half], plus(behind[half:], down).astype(BF16)], axis=0)
    from_behind = neighbour(ahead, axis, 1)
    from_ahead = neighbour(behind, axis, -1)
    return plus(groups(0), from_behind, from_ahead).astype(final)


def scatter_sums(first, second):
    up_a, down_a = far_sums(first, 0)
    up_b, down_b = far_sums(second, 1)
    up_a, down_a, up_b, down_b = lax.optimization_barrier((up_a, down_a, up_b, down_b))
    a = near_sums(first, 0, up_a, down_a, BF16)
    b = near_sums(second, 1, up_b, down_b, BF16)
    first, second = (lambda k: a[k % SIDE]), (lambda k: b[k % SIDE])
    a_last = near_sums(first, 1, *far_sums(first, 1), F32)
    b_last = near_sums(second, 0, *far_sums(second, 0), F32)
    return jnp.concatenate([a_last, b_last], axis=0)


def gather_direct(block, axis):
    return [
        block,
        neighbour(block, axis, -1),
        neighbour(block, axis, 2),
        neighbour(block, axis, 1),
    ]


def gather_rows(rows, beside=None):
    tie = (lambda v: v) if beside is None else lax.optimization_barrier
    part = rows.shape[0] // 2
    a, b = gather_direct(rows[:part], 1), gather_direct(rows[part:], 0)
    a, b = tie((a, b))
    a, b = jnp.stack(a), jnp.stack(b)
    half = a.shape[0] // 2
    a_behind, a_ahead = neighbour(a, 0, 1), neighbour(a, 0, -1)
    b_behind, b_ahead = neighbour(b, 1, 1), neighbour(b, 1, -1)
    a_behind, a_ahead, b_behind, b_ahead, beside = tie(
        (a_behind, a_ahead, b_behind, b_ahead, beside)
    )
    a_far = (neighbour(a_behind[:half], 0, 1), neighbour(a_ahead[half:], 0, -1))
    b_far = (neighbour(b_behind[:half], 1, 1), neighbour(b_ahead[half:], 1, -1))
    first = [a, a_ahead, jnp.concatenate(a_far, axis=0), a_behind]
    second = [b, b_ahead, jnp.concatenate(b_far, axis=0), b_behind]
    return first, second, beside


def along_seq(value, pairs):
    return lax.ppermute(value, "seq", pairs)


def other_core(value):
    return along_seq(value, [(i, i ^ 1) for i in range(lax.axis_size("seq"))])


def relay(total, core):
    mine = total.astype(BF16)
    theirs = other_core(mine)
    early = jnp.where(core == 0, mine, theirs)
    late = jnp.where(core == 0, theirs, mine)
    chip = jnp.einsum("hkl,hlm->hkm", late[:, :, :DK], early, preferred_element_type=F32)
    chip = jnp.concatenate([chip[:, :, :DK], chip[:, :, DK:] + late[:, :, DK:].astype(F32)], axis=2)
    chip = chip.astype(BF16)
    size = lax.axis_size("seq")
    shifts = [along_seq(chip, [(i, i + 2 * d) for i in range(size - 2 * d)]) for d in (3, 2, 1)]
    return jnp.stack(shifts + [theirs])


def local(
    tokens,
    norm_in,
    w_query,
    w_key,
    w_value,
    w_outgate,
    log_decay,
    write_rate,
    head_gain,
    w_output,
    norm_post,
    route_ids,
    route_weights,
    w_gate,
    w_up,
    w_down,
    w_shared_gate,
    w_shared_up,
    w_shared_down,
    w_shared_switch,
):
    tok_dev = tokens.shape[0]
    owners = lax.axis_size("exp")
    tok_seq = tok_dev * owners
    position = lax.axis_index("exp")
    residual_in = tokens.astype(F32)
    normed = row_norm(residual_in, norm_in, 1e-06).astype(BF16)
    y, x = position // SIDE, position % SIDE
    core = lax.axis_index("seq") % 2
    place = jnp.stack([y, x, core]).astype(jnp.int32)
    half = w_output.shape[1] // 2
    w_half = lax.dynamic_slice_in_dim(w_output, core * half, half, 1)
    firsts, seconds, w_half = gather_rows(normed, w_half)
    w_half = lax.all_gather(w_half, "exp", axis=0)
    blocks = tok_seq // BLOCK
    cumulative = jnp.cumsum(log_decay.reshape(2, blocks, BLOCK), axis=-1)
    weights = (w_query, w_key, w_value, w_outgate)
    base, reach, gate, total = delta_local(
        place, firsts, seconds, weights, cumulative, write_rate.reshape(2, blocks, BLOCK)
    )
    maps = relay(total, core)
    gated = delta_gate(place, maps, base, reach, gate, head_gain.reshape(1, DV))
    arrived = lax.all_to_all(
        gated.reshape(owners, tok_dev, -1), "exp", split_axis=0, concat_axis=0, tiled=True
    )
    theirs = other_core(arrived)
    mix = lambda rows: jnp.einsum("stc,scd->td", rows, w_half, preferred_element_type=F32)
    back = other_core(mix(theirs).astype(BF16)).astype(F32)
    kept = mix(arrived)
    mixed_out = jnp.concatenate(
        [jnp.where(core == 0, kept, back), jnp.where(core == 0, back, kept)], axis=1
    )
    residual = residual_in + mixed_out
    post_norm = row_norm(residual, norm_post, 1e-06).astype(BF16)
    rows_first, rows_second, _ = gather_rows(post_norm)
    switch = jax.nn.sigmoid(jnp.dot(post_norm, w_shared_switch, preferred_element_type=F32))
    inner_act = (
        jax.nn.silu(jnp.dot(post_norm, w_shared_gate, preferred_element_type=F32))
        * jnp.dot(post_norm, w_shared_up, preferred_element_type=F32)
    ).astype(BF16)
    shared = jnp.dot(inner_act, w_shared_down, preferred_element_type=F32) * switch[:, None]
    count = w_gate.shape[0]
    mine = position * count + jnp.arange(count, dtype=jnp.int32)
    shares = jnp.sum(
        jnp.where(route_ids[:, :, None] == mine, route_weights[:, :, None], 0.0), axis=1
    )
    shares = jnp.roll(shares.T.reshape(count, SIDE, SIDE, 2, tok_dev // 2), (-y, -x), (1, 2))
    share_first = jnp.transpose(shares[:, :, :, 0], (1, 2, 3, 0))
    share_second = jnp.transpose(shares[:, :, :, 1], (2, 1, 3, 0))
    made = {}
    previous = None
    for k in (0, 1, 2, 3):
        xa, xb = rows_first[k], rows_second[k]
        if previous is None:
            xa, xb, shared = lax.optimization_barrier((xa, xb, shared))
        else:
            xa, xb, *made[previous] = lax.optimization_barrier((xa, xb, *made[previous]))
        made[k] = expert_mix(xa, xb, share_first[k], share_second[k], w_gate, w_up, w_down)
        previous = k
    routed = scatter_sums(lambda k: made[k % SIDE][0], lambda k: made[k % SIDE][1])
    return (residual + shared + routed).astype(BF16)


def solution(mesh):
    in_specs = (
        P(("seq", "exp"), None),
        P(),
        P(None, "exp"),
        P(None, "exp"),
        P(None, "exp"),
        P(None, "exp"),
        P("exp", "seq"),
        P("exp", "seq"),
        P(),
        P("exp", None),
        P(),
        P("seq", None),
        P("seq", None),
        P("exp", None, None),
        P("exp", None, None),
        P("exp", None, None),
        P(),
        P(),
        P(),
        P(),
    )
    out_specs = P(("seq", "exp"), None)
    return jax.shard_map(local, mesh=mesh, in_specs=in_specs, out_specs=out_specs, check_vma=False)
```

```python
import jax
import jax.numpy as jnp
from jax import lax
from jax.experimental import pallas as pl
from jax.experimental.pallas import tpu as pltpu
from jax.sharding import PartitionSpec as P

DK = 128
DV = 128
BLOCK = 128
F32 = jnp.float32
BF16 = jnp.bfloat16
NN = (((1,), (0,)), ((), ()))
NT = (((1,), (1,)), ((), ()))
TN = (((0,), (0,)), ((), ()))


def row_norm(values, gain_vec, epsilon):
    return (
        values * lax.rsqrt(jnp.mean(values * values, axis=-1, keepdims=True) + epsilon) * gain_vec
    )


def split(x):
    hi = x.astype(BF16)
    return hi, (x - hi.astype(F32)).astype(BF16)


def mm(a, b, dims=NN):
    return lax.dot_general(a, b, dims, preferred_element_type=F32)


def dot3_narrow(a, b):
    ah, al = split(a)
    bh, bl = split(b)
    left = jnp.concatenate([ah, al], axis=1)
    right = jnp.concatenate(
        [jnp.concatenate([bh, bl], axis=1), jnp.concatenate([bh, jnp.zeros_like(bl)], axis=1)],
        axis=0,
    )
    both = mm(left, right)
    return both[:, :128] + both[:, 128:]


def dot3_wide(a, b):
    ah, al = split(a)
    bh, bl = split(b)
    return mm(jnp.concatenate([ah, al], axis=1), jnp.concatenate([bh, bh], axis=0)) + mm(ah, bl)


def delta_kernel(
    blocks,
    place_ref,
    *refs,
):
    gathered, refs = refs[: 4 * SIDE], refs[4 * SIDE :]
    query_ref, key_ref, value_ref, outgate_ref, cum_ref, rate_ref = refs[:6]
    base_ref, reach_ref, gate_ref, total_ref, state, held, lines, proj_ref, pair_ref, arrived = refs[6:]
    step = pl.program_id(0)

    @pl.when(step == 0)
    def _():
        copies = [
            pltpu.make_async_copy(
                ref, held.at[i // (2 * SIDE), i // 2 % SIDE, pl.ds(i % 2 * 2, 2)], arrived.at[i]
            )
            for i, ref in enumerate(gathered)
        ]
        for copy in copies:
            copy.start()
        pair_ref[:, :DK] = query_ref[...]
        pair_ref[:, DK:] = key_ref[...]
        for copy in copies:
            copy.wait()

    part = held.shape[3]
    pair = 4

    def project(c, carry):
        for u in range(pair):
            block = c * pair + u
            far_y = lax.rem(step * (blocks // SIDE) + block // SIDE - place_ref[0] + SIDE, SIDE)
            far_x = lax.rem(block % SIDE - place_ref[1] + SIDE, SIDE)
            lines[u * BLOCK : u * BLOCK + part] = held[0, far_y, far_x]
            lines[u * BLOCK + part : (u + 1) * BLOCK] = held[1, far_x, far_y]
        x = lines[...]
        span = pl.ds(pl.multiple_of(c * pair * BLOCK, pair * BLOCK), pair * BLOCK)
        proj_ref[span, : 2 * DK] = mm(x, pair_ref[...])
        proj_ref[span, 2 * DK :] = mm(x, value_ref[...])
        gate_ref[span, :] = mm(x, outgate_ref[...])
        return carry

    lax.fori_loop(0, blocks // pair, project, 0)
    rows = lax.broadcasted_iota(jnp.int32, (BLOCK, BLOCK), 0)
    cols = lax.broadcasted_iota(jnp.int32, (BLOCK, BLOCK), 1)
    causal = rows >= cols
    strict = rows > cols
    apart = rows ^ cols
    eye = jnp.where(rows == cols, 1.0, 0.0).astype(F32)
    heads = 2

    @pl.when(step == 0)
    def _():
        for h in range(heads):
            state[h] = jnp.concatenate([eye, jnp.zeros((DK, DV), F32)], axis=1)

    problems = []
    for b in range(blocks):
        span = slice(b * BLOCK, (b + 1) * BLOCK)
        query = proj_ref[span, 0:DK]
        key = proj_ref[span, DK : 2 * DK]
        key = key * lax.rsqrt(jnp.sum(key * key, axis=-1, keepdims=True) + 1e-06)
        qh, ql = split(query)
        kh, kl = split(key)
        stacked_h = jnp.concatenate([kh, qh], axis=0)
        stacked_l = jnp.concatenate([kl, ql], axis=0)
        products = mm(stacked_h, kh, NT) + (mm(stacked_h, kl, NT) + mm(stacked_l, kh, NT))
        key_key, query_key = products[:BLOCK], products[BLOCK:]
        for h in range(heads):
            cum_row = jnp.broadcast_to(cum_ref[h, b : b + 1, :], (BLOCK, BLOCK))
            rate_row = jnp.broadcast_to(rate_ref[h, b : b + 1, :], (BLOCK, BLOCK))
            cum_col = cum_row.T
            rate_col = rate_row.T
            ratios = jnp.where(causal, jnp.exp(jnp.where(causal, cum_col - cum_row, 0.0)), 0.0)
            weighted = ratios * rate_row
            lower = jnp.where(strict, weighted * key_key, 0.0)
            mixing = weighted * query_key
            decays = jnp.exp(cum_col)
            last = cum_col[BLOCK - 1 : BLOCK, :]
            key_tail = key * (jnp.exp(last - cum_col) * rate_col)
            value = proj_ref[span, 2 * DK + h * DV : 2 * DK + (h + 1) * DV]
            problems.append(
                dict(
                    b=b,
                    h=h,
                    lower=lower,
                    mixing=mixing,
                    right=jnp.concatenate([value, decays * key], axis=1),
                    query=decays * query,
                    key_tail=key_tail,
                    fade=jnp.exp(last) * eye,
                    inverse=eye - jnp.where(apart == 1, lower, 0.0),
                )
            )
    size = 2
    while size < BLOCK:
        for p in problems:
            part = jnp.where((apart >= size) & (apart < 2 * size), p["lower"], 0.0)
            p["inner"] = dot3_narrow(part, p["inverse"])
        for p in problems:
            p["inverse"] = p["inverse"] - dot3_narrow(p["inverse"], p["inner"])
        size *= 2
    for p in problems:
        p["solved"] = dot3_wide(p["inverse"], p["right"])
    for p in problems:
        p["mixed"] = dot3_wide(p["mixing"], p["solved"])
        p["tail"] = dot3_wide(p["key_tail"].T, p["solved"])
    for p in problems:
        h = p["h"]
        span = slice(p["b"] * BLOCK, (p["b"] + 1) * BLOCK)
        cols_h = slice(h * DV, (h + 1) * DV)
        before = state[h]
        effective = p["query"] - p["mixed"][:, DV:]
        seen = dot3_wide(effective, before)
        reach_ref[span, cols_h] = seen[:, :DK]
        base_ref[span, cols_h] = p["mixed"][:, :DV] + seen[:, DK:]
        moved = dot3_wide(p["fade"] - p["tail"][:, DV:], before)
        state[h] = jnp.concatenate([moved[:, :DK], moved[:, DK:] + p["tail"][:, :DV]], axis=1)

    @pl.when(step == pl.num_programs(0) - 1)
    def _():
        total_ref[...] = state[...]


def delta_local(place, firsts, seconds, weights, cumulative, rates):
    pieces = [piece for pair in firsts + seconds for piece in pair]
    side = SIDE
    _, part, width = pieces[0].shape
    tokens = 2 * side * side * part
    blocks = 8
    whole = lambda i, p: (0, 0)
    lines = pl.BlockSpec((blocks * BLOCK, 2 * DV), lambda i, p: (i, 0))
    rates_spec = pl.BlockSpec((2, blocks, BLOCK), lambda i, p: (0, i, 0))
    return pl.pallas_call(
        lambda *refs: delta_kernel(blocks, *refs),
        grid_spec=pltpu.PrefetchScalarGridSpec(
            num_scalar_prefetch=1,
            grid=(tokens // (blocks * BLOCK),),
            in_specs=[pl.BlockSpec(memory_space=pl.ANY)] * (4 * side)
            + [pl.BlockSpec(w.shape, whole, pipeline_mode=pl.Buffered(1)) for w in weights]
            + [rates_spec, rates_spec],
            out_specs=[
                lines,
                lines,
                lines,
                pl.BlockSpec((2, DK, DK + DV), lambda i, p: (0, 0, 0)),
            ],
            scratch_shapes=[
                pltpu.VMEM((2, DK, DK + DV), F32),
                pltpu.VMEM((2, side, side, part, width), BF16),
                pltpu.VMEM((4 * BLOCK, width), BF16),
                pltpu.VMEM((blocks * BLOCK, 2 * DK + 2 * DV), F32),
                pltpu.VMEM((width, 2 * DK), BF16),
                pltpu.SemaphoreType.DMA((4 * side,)),
            ],
        ),
        out_shape=[jax.ShapeDtypeStruct((tokens, 2 * DV), F32)] * 3
        + [jax.ShapeDtypeStruct((2, DK, DK + DV), F32)],
        compiler_params=pltpu.CompilerParams(vmem_limit_bytes=60 * 2**20),
        cost_estimate=pl.CostEstimate(
            flops=3 * 10**10, bytes_accessed=2 * 10**7, transcendentals=0
        ),
        name="delta_local",
    )(place, *pieces, *weights, cumulative, rates)


def gate_kernel(
    place_ref, maps_ref, base_ref, reach_ref, gate_ref, gain_ref, out_ref, entering
):
    @pl.when(pl.program_id(0) == 0)
    def _():
        states = [jnp.zeros((DK, DV), F32)] * 2
        for j in range(maps_ref.shape[0]):
            for h in range(2):
                pair = maps_ref[j, h]
                high, low = split(states[h])
                moved = mm(pair[:, :DK], jnp.concatenate([high, low], axis=1))
                states[h] = moved[:, :DV] + moved[:, DV:] + pair[:, DK:].astype(F32)
                if j == maps_ref.shape[0] - 2:
                    entering[h] = states[h]
        for h in range(2):
            entering[h] = jnp.where(place_ref[2] == 1, states[h], entering[h])

    for h in range(2):
        span = slice(h * DV, (h + 1) * DV)
        attended = base_ref[:, span] + dot3_narrow(reach_ref[:, span], entering[h])
        scaled = row_norm(attended, gain_ref[...], 1e-06)
        u = gate_ref[:, span]
        out_ref[:, span] = (scaled * (u / (1.0 + jnp.exp(-u)))).astype(out_ref.dtype)


def delta_gate(place, maps, base, reach, gate, gain):
    tokens = base.shape[0]
    rows = 512
    lines = pl.BlockSpec((rows, 2 * DV), lambda i, p: (i, 0))
    return pl.pallas_call(
        gate_kernel,
        grid_spec=pltpu.PrefetchScalarGridSpec(
            num_scalar_prefetch=1,
            grid=(tokens // rows,),
            in_specs=[
                pl.BlockSpec(maps.shape, lambda i, p: (0, 0, 0, 0)),
                lines,
                lines,
                lines,
                pl.BlockSpec((1, DV), lambda i, p: (0, 0)),
            ],
            out_specs=lines,
            scratch_shapes=[pltpu.VMEM((2, DK, DV), F32)],
        ),
        out_shape=jax.ShapeDtypeStruct((tokens, 2 * DV), BF16),
        compiler_params=pltpu.CompilerParams(vmem_limit_bytes=60 * 2**20),
        cost_estimate=pl.CostEstimate(flops=10**9, bytes_accessed=10**7, transcendentals=10**6),
        name="delta_gate",
    )(place, maps, base, reach, gate, gain)


def expert_kernel(*refs):
    pieces, (sa_ref, sb_ref, gate_ref, up_ref, down_ref), outs = refs[:4], refs[4:9], refs[9:13]
    x_ref, total = refs[13:]
    width = x_ref.shape[1]
    rows = x_ref.shape[0] // 4
    step = pl.program_id(0)
    expert = step // EXPERT_CUTS

    @pl.when(step == 0)
    def _():
        for i, piece in enumerate(pieces):
            x_ref[i * rows : (i + 1) * rows] = piece[...].reshape(rows, width)

    x = x_ref[...]
    shares = jnp.concatenate(
        [sa_ref[...].reshape(2 * rows, -1), sb_ref[...].reshape(2 * rows, -1)], axis=0
    )
    share = jnp.where(expert == 0, shares[:, 0:1], shares[:, 1:2])
    gated = mm(x, gate_ref[0])
    raised = mm(x, up_ref[0])
    hidden = gated / (1.0 + jnp.exp(-gated)) * raised * share
    made = mm(hidden.astype(BF16), down_ref[0])

    @pl.when(step == 0)
    def _():
        total[...] = made

    @pl.when((step > 0) & (step < pl.num_programs(0) - 1))
    def _():
        total[...] += made

    @pl.when(step == pl.num_programs(0) - 1)
    def _():
        done = (total[...] + made).astype(outs[0].dtype)
        for i, out in enumerate(outs):
            out[...] = done[i * rows : (i + 1) * rows].reshape(out.shape)


EXPERT_CUTS = 2


def expert_mix(xa, xb, sa, sb, w_gate, w_up, w_down):
    pieces = (*xa, *xb)
    _, part, width = pieces[0].shape
    side = SIDE
    count, _, inner = w_gate.shape
    cut = inner // EXPERT_CUTS
    whole = lambda i: (0, 0, 0)
    rows_spec = pl.BlockSpec((2, part, width), whole, pipeline_mode=pl.Buffered(1))
    share_spec = pl.BlockSpec((side, part, count), whole, pipeline_mode=pl.Buffered(1))
    out_spec = pl.BlockSpec((2, part, width), whole)
    across = pl.BlockSpec((1, width, cut), lambda i: (i // EXPERT_CUTS, 0, i % EXPERT_CUTS))
    down = pl.BlockSpec((1, cut, width), lambda i: (i // EXPERT_CUTS, i % EXPERT_CUTS, 0))
    return pl.pallas_call(
        expert_kernel,
        grid=(count * EXPERT_CUTS,),
        in_specs=[rows_spec] * 4 + [share_spec, share_spec, across, across, down],
        out_specs=[out_spec] * 4,
        out_shape=[jax.ShapeDtypeStruct((2, part, width), BF16)] * 4,
        scratch_shapes=[
            pltpu.VMEM((2 * side * part, width), BF16),
            pltpu.VMEM((2 * side * part, width), F32),
        ],
        compiler_params=pltpu.CompilerParams(vmem_limit_bytes=48 * 2**20),
        cost_estimate=pl.CostEstimate(
            flops=12 * side * part * count * width * inner,
            bytes_accessed=6 * count * width * inner + 8 * side * part * width,
            transcendentals=2 * side * part * count * inner,
        ),
        name="expert_mix",
    )(*pieces, sa, sb, w_gate, w_up, w_down)


SIDE = 4


def neighbour(value, axis, by):
    pairs = []
    for y in range(SIDE):
        for x in range(SIDE):
            ny, nx = ((y + by) % SIDE, x) if axis == 0 else (y, (x + by) % SIDE)
            pairs.append((y * SIDE + x, ny * SIDE + nx))
    return lax.ppermute(value, "exp", pairs)


def plus(*terms):
    total = terms[0].astype(F32)
    for term in terms[1:]:
        total = total + term.astype(F32)
    return total


def far_sums(groups, axis):
    early, late = groups(2)
    return neighbour(early, axis, 1), neighbour(late, axis, -1)


def near_sums(groups, axis, up, down):
    own, ahead, behind = groups(0), groups(1), groups(-1)
    behind_late = neighbour(ahead[1], axis, 1)
    ahead_early = neighbour(behind[0], axis, -1)
    behind_early = neighbour(plus(ahead[0], up).astype(BF16), axis, 1)
    ahead_late = neighbour(plus(behind[1], down).astype(BF16), axis, -1)
    return (
        plus(own[0], behind_early, ahead_early).astype(BF16),
        plus(own[1], behind_late, ahead_late).astype(BF16),
    )


def direct_sums(pair, axis):
    terms = [pair[0][0], pair[0][1], pair[1][0], pair[1][1]]
    far = neighbour(terms[2], axis, 2)
    behind = neighbour(terms[1], axis, 1)
    ahead = neighbour(terms[3], axis, -1)
    return plus(terms[0], behind, ahead, far)


def scatter_sums(first, second):
    up_a, down_a = far_sums(first, 0)
    up_b, down_b = far_sums(second, 1)
    up_a, down_a, up_b, down_b = lax.optimization_barrier((up_a, down_a, up_b, down_b))
    a = near_sums(first, 0, up_a, down_a)
    b = near_sums(second, 1, up_b, down_b)
    return jnp.concatenate([direct_sums(a, 1), direct_sums(b, 0)], axis=0)


def gather_direct(block, axis):
    ahead, far, behind = (neighbour(block, axis, by) for by in (-1, 2, 1))
    return jnp.stack([block, ahead]), jnp.stack([far, behind])


def gather_pieces(pair, axis):
    early, late = pair
    behind_early = neighbour(early, axis, 1)
    ahead_late = neighbour(late, axis, -1)
    behind_late = neighbour(late, axis, 1)
    ahead_early = neighbour(early, axis, -1)
    far = (neighbour(behind_early, axis, 1), neighbour(ahead_late, axis, -1))
    return [pair, (ahead_early, ahead_late), far, (behind_early, behind_late)]


def gather_rows(rows, beside=None):
    part = rows.shape[0] // 2
    a, b = gather_direct(rows[:part], 1), gather_direct(rows[part:], 0)
    if beside is not None:
        a, b, beside = lax.optimization_barrier((a, b, beside))
    return gather_pieces(a, 0), gather_pieces(b, 1), beside


def along_seq(value, pairs):
    return lax.ppermute(value, "seq", pairs)


def other_core(value):
    return along_seq(value, [(i, i ^ 1) for i in range(lax.axis_size("seq"))])


def relay(total, core):
    mine = total.astype(BF16)
    theirs = other_core(mine)
    early = jnp.where(core == 0, mine, theirs)
    late = jnp.where(core == 0, theirs, mine)
    chip = jnp.einsum("hkl,hlm->hkm", late[:, :, :DK], early, preferred_element_type=F32)
    chip = jnp.concatenate([chip[:, :, :DK], chip[:, :, DK:] + late[:, :, DK:].astype(F32)], axis=2)
    chip = chip.astype(BF16)
    size = lax.axis_size("seq")
    shifts = [along_seq(chip, [(i, i + 2 * d) for i in range(size - 2 * d)]) for d in (3, 2, 1)]
    return jnp.stack(shifts + [theirs])


def local(
    tokens,
    norm_in,
    w_query,
    w_key,
    w_value,
    w_outgate,
    log_decay,
    write_rate,
    head_gain,
    w_output,
    norm_post,
    route_ids,
    route_weights,
    w_gate,
    w_up,
    w_down,
    w_shared_gate,
    w_shared_up,
    w_shared_down,
    w_shared_switch,
):
    tok_dev = tokens.shape[0]
    owners = lax.axis_size("exp")
    tok_seq = tok_dev * owners
    position = lax.axis_index("exp")
    residual_in = tokens.astype(F32)
    normed = row_norm(residual_in, norm_in, 1e-06).astype(BF16)
    y, x = position // SIDE, position % SIDE
    core = lax.axis_index("seq") % 2
    place = jnp.stack([y, x, core]).astype(jnp.int32)
    chips = lax.axis_size("seq") // 2
    piece = w_output.shape[1] // (2 * chips)
    w_piece = lax.dynamic_slice_in_dim(
        w_output, (core * chips + lax.axis_index("seq") // 2) * piece, piece, 1
    )
    w_piece = lax.all_gather(w_piece, "exp", axis=0, tiled=True)
    firsts, seconds, w_piece = gather_rows(normed, w_piece)
    same_core = [[2 * i + c for i in range(chips)] for c in range(2)]
    w_half = lax.all_gather(w_piece, "seq", axis=0, axis_index_groups=same_core)
    blocks = tok_seq // BLOCK
    cumulative = jnp.cumsum(log_decay.reshape(2, blocks, BLOCK), axis=-1)
    weights = (w_query, w_key, w_value, w_outgate)
    base, reach, gate, total = delta_local(
        place, firsts, seconds, weights, cumulative, write_rate.reshape(2, blocks, BLOCK)
    )
    maps = relay(total, core)
    gated = delta_gate(place, maps, base, reach, gate, head_gain.reshape(1, DV))
    arrived = lax.all_to_all(
        gated.reshape(owners, tok_dev, -1), "exp", split_axis=0, concat_axis=0, tiled=True
    )
    theirs = other_core(arrived)

    def mix(rows):
        rows = jnp.transpose(rows, (1, 0, 2)).reshape(tok_dev, -1)
        return jnp.concatenate(
            [jnp.dot(rows, w_half[i], preferred_element_type=F32) for i in range(chips)], axis=1
        )

    back = other_core(mix(theirs).astype(BF16)).astype(F32)
    kept = mix(arrived)
    mixed_out = jnp.concatenate(
        [jnp.where(core == 0, kept, back), jnp.where(core == 0, back, kept)], axis=1
    )
    residual = residual_in + mixed_out
    post_norm = row_norm(residual, norm_post, 1e-06).astype(BF16)
    rows_first, rows_second, _ = gather_rows(post_norm)
    switch = jax.nn.sigmoid(jnp.dot(post_norm, w_shared_switch, preferred_element_type=F32))
    inner_act = (
        jax.nn.silu(jnp.dot(post_norm, w_shared_gate, preferred_element_type=F32))
        * jnp.dot(post_norm, w_shared_up, preferred_element_type=F32)
    ).astype(BF16)
    shared = jnp.dot(inner_act, w_shared_down, preferred_element_type=F32) * switch[:, None]
    count = w_gate.shape[0]
    mine = position * count + jnp.arange(count, dtype=jnp.int32)
    shares = jnp.sum(
        jnp.where(route_ids[:, :, None] == mine, route_weights[:, :, None], 0.0), axis=1
    )
    shares = jnp.roll(shares.T.reshape(count, SIDE, SIDE, 2, tok_dev // 2), (-y, -x), (1, 2))
    share_first = jnp.transpose(shares[:, :, :, 0], (1, 2, 3, 0))
    share_second = jnp.transpose(shares[:, :, :, 1], (2, 1, 3, 0))
    made = {}
    previous = shared
    for k in (0, 1, 2, 3):
        xa, xb = rows_first[k], rows_second[k]
        xa, xb, previous = lax.optimization_barrier((xa, xb, previous))
        if k == 0:
            shared = previous
        else:
            made[k - 1] = previous
        previous = expert_mix(xa, xb, share_first[k], share_second[k], w_gate, w_up, w_down)
    made[3] = previous
    routed = scatter_sums(lambda k: made[k % SIDE][:2], lambda k: made[k % SIDE][2:])
    return (residual + shared + routed).astype(BF16)


def solution(mesh):
    in_specs = (
        P(("seq", "exp"), None),
        P(),
        P(None, "exp"),
        P(None, "exp"),
        P(None, "exp"),
        P(None, "exp"),
        P("exp", "seq"),
        P("exp", "seq"),
        P(),
        P("exp", None),
        P(),
        P("seq", None),
        P("seq", None),
        P("exp", None, None),
        P("exp", None, None),
        P("exp", None, None),
        P(),
        P(),
        P(),
        P(),
    )
    out_specs = P(("seq", "exp"), None)
    return jax.shard_map(local, mesh=mesh, in_specs=in_specs, out_specs=out_specs, check_vma=False)
```

```python
import jax
import jax.numpy as jnp
from jax import lax
from jax.experimental import pallas as pl
from jax.experimental.pallas import tpu as pltpu
from jax.sharding import PartitionSpec as P

DK = 128
DV = 128
BLOCK = 128
F32 = jnp.float32
BF16 = jnp.bfloat16
NN = (((1,), (0,)), ((), ()))
NT = (((1,), (1,)), ((), ()))
TN = (((0,), (0,)), ((), ()))


def row_norm(values, gain_vec, epsilon):
    return (
        values * lax.rsqrt(jnp.mean(values * values, axis=-1, keepdims=True) + epsilon) * gain_vec
    )


def split(x):
    hi = x.astype(BF16)
    return hi, (x - hi.astype(F32)).astype(BF16)


def mm(a, b, dims=NN):
    return lax.dot_general(a, b, dims, preferred_element_type=F32)


def dot3_narrow(a, b):
    ah, al = split(a)
    bh, bl = split(b)
    left = jnp.concatenate([ah, al], axis=1)
    right = jnp.concatenate(
        [jnp.concatenate([bh, bl], axis=1), jnp.concatenate([bh, jnp.zeros_like(bl)], axis=1)],
        axis=0,
    )
    both = mm(left, right)
    return both[:, :128] + both[:, 128:]


def dot3_wide(a, b):
    ah, al = split(a)
    bh, bl = split(b)
    return mm(jnp.concatenate([ah, al], axis=1), jnp.concatenate([bh, bh], axis=0)) + mm(ah, bl)


def delta_kernel(blocks, spots, place_ref, *refs):
    gathered, refs = refs[: len(spots)], refs[len(spots) :]
    query_ref, key_ref, value_ref, outgate_ref, cum_ref, rate_ref = refs[:6]
    base_ref, reach_ref, gate_ref, total_ref, state, held, lines, proj_ref, pair_ref, arrived = refs[6:]
    step = pl.program_id(0)

    @pl.when(step == 0)
    def _():
        copies = [
            pltpu.make_async_copy(ref, held.at[group, away, pl.ds(start, count)], arrived.at[i])
            for i, (ref, (group, away, start, count)) in enumerate(zip(gathered, spots))
        ]
        for copy in copies:
            copy.start()
        pair_ref[:, :DK] = query_ref[...]
        pair_ref[:, DK:] = key_ref[...]
        for copy in copies:
            copy.wait()

    part = held.shape[3]
    pair = 4

    def project(c, carry):
        for u in range(pair):
            block = c * pair + u
            far_y = lax.rem(step * (blocks // SIDE) + block // SIDE - place_ref[0] + SIDE, SIDE)
            far_x = lax.rem(block % SIDE - place_ref[1] + SIDE, SIDE)
            lines[u * BLOCK : u * BLOCK + part] = held[0, far_y, far_x]
            lines[u * BLOCK + part : (u + 1) * BLOCK] = held[1, far_x, far_y]
        x = lines[...]
        span = pl.ds(pl.multiple_of(c * pair * BLOCK, pair * BLOCK), pair * BLOCK)
        proj_ref[span, : 2 * DK] = mm(x, pair_ref[...])
        proj_ref[span, 2 * DK :] = mm(x, value_ref[...])
        gate_ref[span, :] = mm(x, outgate_ref[...])
        return carry

    lax.fori_loop(0, blocks // pair, project, 0)
    rows = lax.broadcasted_iota(jnp.int32, (BLOCK, BLOCK), 0)
    cols = lax.broadcasted_iota(jnp.int32, (BLOCK, BLOCK), 1)
    causal = rows >= cols
    strict = rows > cols
    apart = rows ^ cols
    eye = jnp.where(rows == cols, 1.0, 0.0).astype(F32)
    heads = 2

    @pl.when(step == 0)
    def _():
        for h in range(heads):
            state[h] = jnp.concatenate([eye, jnp.zeros((DK, DV), F32)], axis=1)

    problems = []
    for b in range(blocks):
        span = slice(b * BLOCK, (b + 1) * BLOCK)
        query = proj_ref[span, 0:DK]
        key = proj_ref[span, DK : 2 * DK]
        key = key * lax.rsqrt(jnp.sum(key * key, axis=-1, keepdims=True) + 1e-06)
        qh, ql = split(query)
        kh, kl = split(key)
        stacked_h = jnp.concatenate([kh, qh], axis=0)
        stacked_l = jnp.concatenate([kl, ql], axis=0)
        products = mm(stacked_h, kh, NT) + (mm(stacked_h, kl, NT) + mm(stacked_l, kh, NT))
        key_key, query_key = products[:BLOCK], products[BLOCK:]
        for h in range(heads):
            cum_row = jnp.broadcast_to(cum_ref[h, b : b + 1, :], (BLOCK, BLOCK))
            rate_row = jnp.broadcast_to(rate_ref[h, b : b + 1, :], (BLOCK, BLOCK))
            cum_col = cum_row.T
            rate_col = rate_row.T
            ratios = jnp.where(causal, jnp.exp(jnp.where(causal, cum_col - cum_row, 0.0)), 0.0)
            weighted = ratios * rate_row
            lower = jnp.where(strict, weighted * key_key, 0.0)
            mixing = weighted * query_key
            decays = jnp.exp(cum_col)
            last = cum_col[BLOCK - 1 : BLOCK, :]
            key_tail = key * (jnp.exp(last - cum_col) * rate_col)
            value = proj_ref[span, 2 * DK + h * DV : 2 * DK + (h + 1) * DV]
            problems.append(
                dict(
                    b=b,
                    h=h,
                    lower=lower,
                    mixing=mixing,
                    right=jnp.concatenate([value, decays * key], axis=1),
                    query=decays * query,
                    key_tail=key_tail,
                    fade=jnp.exp(last) * eye,
                    inverse=eye - jnp.where(apart == 1, lower, 0.0),
                )
            )
    size = 2
    while size < BLOCK:
        for p in problems:
            part = jnp.where((apart >= size) & (apart < 2 * size), p["lower"], 0.0)
            p["inner"] = dot3_narrow(part, p["inverse"])
        for p in problems:
            p["inverse"] = p["inverse"] - dot3_narrow(p["inverse"], p["inner"])
        size *= 2
    for p in problems:
        p["solved"] = dot3_wide(p["inverse"], p["right"])
    for p in problems:
        p["mixed"] = dot3_wide(p["mixing"], p["solved"])
        p["tail"] = dot3_wide(p["key_tail"].T, p["solved"])
    for p in problems:
        h = p["h"]
        span = slice(p["b"] * BLOCK, (p["b"] + 1) * BLOCK)
        cols_h = slice(h * DV, (h + 1) * DV)
        before = state[h]
        effective = p["query"] - p["mixed"][:, DV:]
        seen = dot3_wide(effective, before)
        reach_ref[span, cols_h] = seen[:, :DK]
        base_ref[span, cols_h] = p["mixed"][:, :DV] + seen[:, DK:]
        moved = dot3_wide(p["fade"] - p["tail"][:, DV:], before)
        state[h] = jnp.concatenate([moved[:, :DK], moved[:, DK:] + p["tail"][:, :DV]], axis=1)

    @pl.when(step == pl.num_programs(0) - 1)
    def _():
        total_ref[...] = state[...]


def delta_local(place, firsts, seconds, weights, cumulative, rates):
    pieces, spots = [], []
    for group, blocks in enumerate((firsts, seconds)):
        for away, parts in enumerate(blocks):
            start = 0
            for piece in parts:
                pieces.append(piece)
                spots.append((group, away, start, piece.shape[0]))
                start += piece.shape[0]
    side = SIDE
    _, part, width = pieces[0].shape
    tokens = 2 * side * side * part
    blocks = 8
    whole = lambda i, p: (0, 0)
    lines = pl.BlockSpec((blocks * BLOCK, 2 * DV), lambda i, p: (i, 0))
    rates_spec = pl.BlockSpec((2, blocks, BLOCK), lambda i, p: (0, i, 0))
    return pl.pallas_call(
        lambda *refs: delta_kernel(blocks, spots, *refs),
        grid_spec=pltpu.PrefetchScalarGridSpec(
            num_scalar_prefetch=1,
            grid=(tokens // (blocks * BLOCK),),
            in_specs=[pl.BlockSpec(memory_space=pl.ANY)] * len(pieces)
            + [pl.BlockSpec(w.shape, whole, pipeline_mode=pl.Buffered(1)) for w in weights]
            + [rates_spec, rates_spec],
            out_specs=[
                lines,
                lines,
                lines,
                pl.BlockSpec((2, DK, DK + DV), lambda i, p: (0, 0, 0)),
            ],
            scratch_shapes=[
                pltpu.VMEM((2, DK, DK + DV), F32),
                pltpu.VMEM((2, side, side, part, width), BF16),
                pltpu.VMEM((4 * BLOCK, width), BF16),
                pltpu.VMEM((blocks * BLOCK, 2 * DK + 2 * DV), F32),
                pltpu.VMEM((width, 2 * DK), BF16),
                pltpu.SemaphoreType.DMA((len(pieces),)),
            ],
        ),
        out_shape=[jax.ShapeDtypeStruct((tokens, 2 * DV), F32)] * 3
        + [jax.ShapeDtypeStruct((2, DK, DK + DV), F32)],
        compiler_params=pltpu.CompilerParams(vmem_limit_bytes=60 * 2**20),
        cost_estimate=pl.CostEstimate(
            flops=3 * 10**10, bytes_accessed=2 * 10**7, transcendentals=0
        ),
        name="delta_local",
    )(place, *pieces, *weights, cumulative, rates)


def gate_kernel(
    place_ref, maps_ref, base_ref, reach_ref, gate_ref, gain_ref, out_ref, entering
):
    @pl.when(pl.program_id(0) == 0)
    def _():
        states = [jnp.zeros((DK, DV), F32)] * 2
        for j in range(maps_ref.shape[0]):
            for h in range(2):
                pair = maps_ref[j, h]
                high, low = split(states[h])
                moved = mm(pair[:, :DK], jnp.concatenate([high, low], axis=1))
                states[h] = moved[:, :DV] + moved[:, DV:] + pair[:, DK:].astype(F32)
                if j == maps_ref.shape[0] - 2:
                    entering[h] = states[h]
        for h in range(2):
            entering[h] = jnp.where(place_ref[2] == 1, states[h], entering[h])

    for h in range(2):
        span = slice(h * DV, (h + 1) * DV)
        attended = base_ref[:, span] + dot3_narrow(reach_ref[:, span], entering[h])
        scaled = row_norm(attended, gain_ref[...], 1e-06)
        u = gate_ref[:, span]
        out_ref[:, span] = (scaled * (u / (1.0 + jnp.exp(-u)))).astype(out_ref.dtype)


def delta_gate(place, maps, base, reach, gate, gain):
    tokens = base.shape[0]
    rows = 512
    lines = pl.BlockSpec((rows, 2 * DV), lambda i, p: (i, 0))
    return pl.pallas_call(
        gate_kernel,
        grid_spec=pltpu.PrefetchScalarGridSpec(
            num_scalar_prefetch=1,
            grid=(tokens // rows,),
            in_specs=[
                pl.BlockSpec(maps.shape, lambda i, p: (0, 0, 0, 0)),
                lines,
                lines,
                lines,
                pl.BlockSpec((1, DV), lambda i, p: (0, 0)),
            ],
            out_specs=lines,
            scratch_shapes=[pltpu.VMEM((2, DK, DV), F32)],
        ),
        out_shape=jax.ShapeDtypeStruct((tokens, 2 * DV), BF16),
        compiler_params=pltpu.CompilerParams(vmem_limit_bytes=60 * 2**20),
        cost_estimate=pl.CostEstimate(flops=10**9, bytes_accessed=10**7, transcendentals=10**6),
        name="delta_gate",
    )(place, maps, base, reach, gate, gain)


def expert_kernel(xa_ref, xb_ref, sa_ref, sb_ref, gate_ref, up_ref, down_ref, oa_ref, ob_ref, x_ref, total):
    width = xa_ref.shape[-1]
    rows = xa_ref.size // width
    step = pl.program_id(0)
    expert = step // EXPERT_CUTS

    @pl.when(step == 0)
    def _():
        x_ref[:rows] = xa_ref[...].reshape(rows, width)
        x_ref[rows:] = xb_ref[...].reshape(rows, width)

    x = x_ref[...]
    shares = jnp.concatenate(
        [sa_ref[...].reshape(rows, -1), sb_ref[...].reshape(rows, -1)], axis=0
    )
    share = jnp.where(expert == 0, shares[:, 0:1], shares[:, 1:2])
    gated = mm(x, gate_ref[0])
    raised = mm(x, up_ref[0])
    hidden = gated / (1.0 + jnp.exp(-gated)) * raised * share
    made = mm(hidden.astype(BF16), down_ref[0])

    @pl.when(step == 0)
    def _():
        total[...] = made

    @pl.when((step > 0) & (step < pl.num_programs(0) - 1))
    def _():
        total[...] += made

    @pl.when(step == pl.num_programs(0) - 1)
    def _():
        done = (total[...] + made).astype(oa_ref.dtype)
        oa_ref[...] = done[:rows].reshape(oa_ref.shape)
        ob_ref[...] = done[rows:].reshape(ob_ref.shape)


EXPERT_CUTS = 2


def expert_mix(xa, xb, sa, sb, w_gate, w_up, w_down):
    side, part, width = xa.shape
    count, _, inner = w_gate.shape
    cut = inner // EXPERT_CUTS
    whole = lambda i: (0, 0, 0)
    rows_spec = pl.BlockSpec((side, part, width), whole, pipeline_mode=pl.Buffered(1))
    share_spec = pl.BlockSpec((side, part, count), whole, pipeline_mode=pl.Buffered(1))
    out_spec = pl.BlockSpec((side, part, width), whole)
    across = pl.BlockSpec((1, width, cut), lambda i: (i // EXPERT_CUTS, 0, i % EXPERT_CUTS))
    down = pl.BlockSpec((1, cut, width), lambda i: (i // EXPERT_CUTS, i % EXPERT_CUTS, 0))
    return pl.pallas_call(
        expert_kernel,
        grid=(count * EXPERT_CUTS,),
        in_specs=[rows_spec, rows_spec, share_spec, share_spec, across, across, down],
        out_specs=[out_spec, out_spec],
        out_shape=[jax.ShapeDtypeStruct((side, part, width), BF16)] * 2,
        scratch_shapes=[
            pltpu.VMEM((2 * side * part, width), BF16),
            pltpu.VMEM((2 * side * part, width), F32),
        ],
        compiler_params=pltpu.CompilerParams(vmem_limit_bytes=48 * 2**20),
        cost_estimate=pl.CostEstimate(
            flops=12 * side * part * count * width * inner,
            bytes_accessed=6 * count * width * inner + 8 * side * part * width,
            transcendentals=2 * side * part * count * inner,
        ),
        name="expert_mix",
    )(xa, xb, sa, sb, w_gate, w_up, w_down)


SIDE = 4


def neighbour(value, axis, by):
    pairs = []
    for y in range(SIDE):
        for x in range(SIDE):
            ny, nx = ((y + by) % SIDE, x) if axis == 0 else (y, (x + by) % SIDE)
            pairs.append((y * SIDE + x, ny * SIDE + nx))
    return lax.ppermute(value, "exp", pairs)


def plus(*terms):
    total = terms[0].astype(F32)
    for term in terms[1:]:
        total = total + term.astype(F32)
    return total


def far_sums(groups, axis):
    far = groups(2)
    half = far.shape[0] // 2
    return neighbour(far[:half], axis, 1), neighbour(far[half:], axis, -1)


def near_sums(groups, axis, up, down, final):
    half = up.shape[0]
    ahead, behind = groups(1), groups(-1)
    ahead = jnp.concatenate([plus(ahead[:half], up).astype(BF16), ahead[half:]], axis=0)
    behind = jnp.concatenate([behind[:half], plus(behind[half:], down).astype(BF16)], axis=0)
    from_behind = neighbour(ahead, axis, 1)
    from_ahead = neighbour(behind, axis, -1)
    return plus(groups(0), from_behind, from_ahead).astype(final)


def direct_sums(terms, axis):
    far = neighbour(terms[2], axis, 2)
    behind = neighbour(terms[1], axis, 1)
    ahead = neighbour(terms[3], axis, -1)
    return plus(terms[0], behind, ahead, far)


def scatter_sums(first, second):
    up_a, down_a = far_sums(first, 0)
    up_b, down_b = far_sums(second, 1)
    up_a, down_a, up_b, down_b = lax.optimization_barrier((up_a, down_a, up_b, down_b))
    a = near_sums(first, 0, up_a, down_a, BF16)
    b = near_sums(second, 1, up_b, down_b, BF16)
    return jnp.concatenate([direct_sums(a, 1), direct_sums(b, 0)], axis=0)


def gather_direct(block, axis):
    return [
        block,
        neighbour(block, axis, -1),
        neighbour(block, axis, 2),
        neighbour(block, axis, 1),
    ]


def gather_rows(rows, beside=None):
    tie = (lambda v: v) if beside is None else lax.optimization_barrier
    part = rows.shape[0] // 2
    a, b = gather_direct(rows[:part], 1), gather_direct(rows[part:], 0)
    a, b = tie((a, b))
    a, b = jnp.stack(a), jnp.stack(b)
    half = a.shape[0] // 2
    a_behind, a_ahead = neighbour(a, 0, 1), neighbour(a, 0, -1)
    b_behind, b_ahead = neighbour(b, 1, 1), neighbour(b, 1, -1)
    a_behind, a_ahead, b_behind, b_ahead = tie((a_behind, a_ahead, b_behind, b_ahead))
    a_far = (neighbour(a_behind[:half], 0, 1), neighbour(a_ahead[half:], 0, -1))
    b_far = (neighbour(b_behind[:half], 1, 1), neighbour(b_ahead[half:], 1, -1))
    a_far, b_far, beside = tie((a_far, b_far, beside))
    first = [(a,), (a_ahead,), a_far, (a_behind,)]
    second = [(b,), (b_ahead,), b_far, (b_behind,)]
    return first, second, beside


def along_seq(value, pairs):
    return lax.ppermute(value, "seq", pairs)


def other_core(value):
    return along_seq(value, [(i, i ^ 1) for i in range(lax.axis_size("seq"))])


def relay(total, core):
    mine = total.astype(BF16)
    theirs = other_core(mine)
    early = jnp.where(core == 0, mine, theirs)
    late = jnp.where(core == 0, theirs, mine)
    chip = jnp.einsum("hkl,hlm->hkm", late[:, :, :DK], early, preferred_element_type=F32)
    chip = jnp.concatenate([chip[:, :, :DK], chip[:, :, DK:] + late[:, :, DK:].astype(F32)], axis=2)
    chip = chip.astype(BF16)
    size = lax.axis_size("seq")
    shifts = [along_seq(chip, [(i, i + 2 * d) for i in range(size - 2 * d)]) for d in (3, 2, 1)]
    return jnp.stack(shifts + [theirs])


def local(
    tokens,
    norm_in,
    w_query,
    w_key,
    w_value,
    w_outgate,
    log_decay,
    write_rate,
    head_gain,
    w_output,
    norm_post,
    route_ids,
    route_weights,
    w_gate,
    w_up,
    w_down,
    w_shared_gate,
    w_shared_up,
    w_shared_down,
    w_shared_switch,
):
    tok_dev = tokens.shape[0]
    owners = lax.axis_size("exp")
    tok_seq = tok_dev * owners
    position = lax.axis_index("exp")
    residual_in = tokens.astype(F32)
    normed = row_norm(residual_in, norm_in, 1e-06).astype(BF16)
    y, x = position // SIDE, position % SIDE
    core = lax.axis_index("seq") % 2
    place = jnp.stack([y, x, core]).astype(jnp.int32)
    half = w_output.shape[1] // 2
    w_half = lax.dynamic_slice_in_dim(w_output, core * half, half, 1)
    firsts, seconds, w_half = gather_rows(normed, w_half)
    w_half = lax.all_gather(w_half, "exp", axis=0)
    blocks = tok_seq // BLOCK
    cumulative = jnp.cumsum(log_decay.reshape(2, blocks, BLOCK), axis=-1)
    weights = (w_query, w_key, w_value, w_outgate)
    base, reach, gate, total = delta_local(
        place, firsts, seconds, weights, cumulative, write_rate.reshape(2, blocks, BLOCK)
    )
    maps = relay(total, core)
    gated = delta_gate(place, maps, base, reach, gate, head_gain.reshape(1, DV))
    arrived = lax.all_to_all(
        gated.reshape(owners, tok_dev, -1), "exp", split_axis=0, concat_axis=0, tiled=True
    )
    theirs = other_core(arrived)
    mix = lambda rows: jnp.einsum("stc,scd->td", rows, w_half, preferred_element_type=F32)
    back = other_core(mix(theirs).astype(BF16)).astype(F32)
    kept = mix(arrived)
    mixed_out = jnp.concatenate(
        [jnp.where(core == 0, kept, back), jnp.where(core == 0, back, kept)], axis=1
    )
    residual = residual_in + mixed_out
    post_norm = row_norm(residual, norm_post, 1e-06).astype(BF16)
    rows_first, rows_second, _ = gather_rows(post_norm)
    switch = jax.nn.sigmoid(jnp.dot(post_norm, w_shared_switch, preferred_element_type=F32))
    inner_act = (
        jax.nn.silu(jnp.dot(post_norm, w_shared_gate, preferred_element_type=F32))
        * jnp.dot(post_norm, w_shared_up, preferred_element_type=F32)
    ).astype(BF16)
    shared = jnp.dot(inner_act, w_shared_down, preferred_element_type=F32) * switch[:, None]
    count = w_gate.shape[0]
    mine = position * count + jnp.arange(count, dtype=jnp.int32)
    shares = jnp.sum(
        jnp.where(route_ids[:, :, None] == mine, route_weights[:, :, None], 0.0), axis=1
    )
    shares = jnp.roll(shares.T.reshape(count, SIDE, SIDE, 2, tok_dev // 2), (-y, -x), (1, 2))
    share_first = jnp.transpose(shares[:, :, :, 0], (1, 2, 3, 0))
    share_second = jnp.transpose(shares[:, :, :, 1], (2, 1, 3, 0))
    made = {}
    previous = None
    for k in (0, 1, 2, 3):
        xa, xb = jnp.concatenate(rows_first[k]), jnp.concatenate(rows_second[k])
        if previous is None:
            xa, xb, shared = lax.optimization_barrier((xa, xb, shared))
        else:
            xa, xb, *made[previous] = lax.optimization_barrier((xa, xb, *made[previous]))
        made[k] = expert_mix(xa, xb, share_first[k], share_second[k], w_gate, w_up, w_down)
        previous = k
    routed = scatter_sums(lambda k: made[k % SIDE][0], lambda k: made[k % SIDE][1])
    return (residual + shared + routed).astype(BF16)


def solution(mesh):
    in_specs = (
        P(("seq", "exp"), None),
        P(),
        P(None, "exp"),
        P(None, "exp"),
        P(None, "exp"),
        P(None, "exp"),
        P("exp", "seq"),
        P("exp", "seq"),
        P(),
        P("exp", None),
        P(),
        P("seq", None),
        P("seq", None),
        P("exp", None, None),
        P("exp", None, None),
        P("exp", None, None),
        P(),
        P(),
        P(),
        P(),
    )
    out_specs = P(("seq", "exp"), None)
    return jax.shard_map(local, mesh=mesh, in_specs=in_specs, out_specs=out_specs, check_vma=False)
```
